256 devices in a mesh: row: 8 (over z), col: 32 (over y, x, core).
Axes of the slice: x: 4, y: 4, z: 8, core: 2. Of those that a mesh axis runs over, the one named last changes fastest.
Arguments:
- blocks: bfloat16 [8, 32, 96, 128, 128], P('row', 'col')
- positions: int32 [8, 32, 96], P('row', 'col'), may hold values from 0 to 255, as said below
- counts: int32 [8, 32], P('row', 'col'), may hold values from 24 to 96, as said below
- sketch: bfloat16 [32768, 288], P(('col', 'row')), may hold values from -6 to 6
Outputs:
- basis: float32 [32768, 288], P(('row', 'col'))
- projected: float32 [32768, 288], P(('col', 'row'))
The draws below stay inside these ranges and needn't reach their ends.
Inputs may be any that keep to these rules, and one draw needn't show every extreme that they name: `positions`: within one device the 96 slots hold distinct places p, each naming block row p // 8 and block column p % 8 of the device's grid. `counts`: slots from a device's count onward are unused.
All inputs are finite; a program needn't handle non-finite values.
Results may differ from the reference program's by a relative error of at most 0.0026.
The reference program's roundings to bfloat16 on the way count: a program that leaves them out, or rounds other values in their place, can miss the bound.
Values may be sent and summed in bfloat16 or wider, within the bound.
A program may use at most 128 MiB of HBM per device.

```python
import math
import jax
import jax.numpy as jnp
from jax import lax

BLOCK = 128
WIDTH = 288
NBR = 32
NBC = 8
KMAX = 96
NORDER = 32768
N_ROW = 8
N_COL = 32


def draw_blocks(key, part):
    key = jax.random.fold_in(key, 13)
    shape = (N_ROW, N_COL, KMAX, BLOCK, BLOCK)
    key_value, key_rows, key_cols = jax.random.split(key, 3)
    values = jax.random.normal(key_value, shape, jnp.float32)
    row_scale = jnp.exp(jax.random.uniform(key_rows, (N_ROW, N_COL, KMAX, BLOCK, 1), jnp.float32, 0.0, math.log(10.0)))
    col_scale = jnp.exp(jax.random.uniform(key_cols, (N_ROW, N_COL, KMAX, 1, BLOCK), jnp.float32, 0.0, math.log(10.0)))
    factor = 1.0 / (21.5 * math.sqrt(KMAX * BLOCK * 5.0 / 8.0))
    return (values * row_scale * col_scale * factor).astype(jnp.bfloat16)


def draw_positions(key, part):
    key = jax.random.fold_in(key, 11)
    keys = jax.random.split(key, N_ROW * N_COL)
    orders = jax.vmap(lambda single: jax.random.permutation(single, NBR * NBC))(keys)
    return orders[:, :KMAX].reshape(N_ROW, N_COL, KMAX).astype(jnp.int32)


def draw_counts(key, part):
    key = jax.random.fold_in(key, 12)
    values = jax.random.randint(key, (N_ROW, N_COL), KMAX // 4, KMAX + 1, dtype=jnp.int32)
    values = values.at[N_ROW - 1, N_COL - 1].set(KMAX // 4)
    values = values.at[0, 0].set(KMAX)
    return values


def block_scale(key, shape, cuts, low, largest):
    level = 1.0
    for axis_at, shards_of in cuts:
        steps = jax.random.uniform(jax.random.fold_in(jax.random.fold_in(key, 6), axis_at), (shards_of,), jnp.float32, low / len(cuts), largest / len(cuts))
        level = level * jnp.repeat(jnp.exp(steps), shape[axis_at] // shards_of).reshape((-1,) + (1,) * (len(shape) - 1 - axis_at))
    return level


def normal_values(stream_key, extent, deviation, reach, cuts=(), held_as=jnp.bfloat16):
    array = deviation * jax.random.normal(stream_key, extent, jnp.float32)
    if cuts:
        array = array * block_scale(stream_key, extent, cuts, -0.22, 0.18)
    return jnp.clip(array, -reach, reach).astype(held_as)


def setup_inputs(seed: int = 0) -> dict:
    seeds = jax.random.split(jax.random.key(seed), 5)
    blocks = draw_blocks(jax.random.fold_in(seeds[4], 71), 0)
    positions = draw_positions(jax.random.fold_in(seeds[4], 71), 0)
    counts = draw_counts(jax.random.fold_in(seeds[4], 71), 0)
    sketch = normal_values(seeds[3], (NORDER, WIDTH), 1.0, 6.0, ((0, 256),))
    return {"blocks": blocks, "positions": positions, "counts": counts, "sketch": sketch}


def spread(blocks, positions, counts, operand, back):
    width = operand.shape[1]
    rows_blk = NBR * BLOCK
    cols_blk = NBC * BLOCK
    slot = jnp.arange(KMAX, dtype=jnp.int32)

    def visit(index, total):
        index = jnp.asarray(index).astype(jnp.int32)
        rpos = index // N_COL
        cpos = index % N_COL
        tiles = blocks[rpos, cpos].astype(jnp.float32)
        places = positions[rpos, cpos]
        used = slot < counts[rpos, cpos]
        brow = places // NBC
        bcol = places % NBC
        if back:
            source = lax.dynamic_slice_in_dim(operand, (rpos * rows_blk).astype(jnp.int32), rows_blk, 0)
            parts = jnp.take(source.reshape(NBR, BLOCK, width), brow, axis=0).astype(jnp.float32)
            prod = jnp.einsum('kji,kjw->kiw', tiles, parts, precision=lax.Precision.HIGHEST)
            onehot = ((bcol[None, :] == jnp.arange(NBC, dtype=jnp.int32)[:, None]) & used[None, :]).astype(jnp.float32)
            result = jnp.einsum('ck,kiw->ciw', onehot, prod, precision=lax.Precision.HIGHEST).reshape(cols_blk, width)
            start = (cpos * cols_blk).astype(jnp.int32)
        else:
            source = lax.dynamic_slice_in_dim(operand, (cpos * cols_blk).astype(jnp.int32), cols_blk, 0)
            parts = jnp.take(source.reshape(NBC, BLOCK, width), bcol, axis=0).astype(jnp.float32)
            prod = jnp.einsum('kij,kjw->kiw', tiles, parts, precision=lax.Precision.HIGHEST)
            onehot = ((brow[None, :] == jnp.arange(NBR, dtype=jnp.int32)[:, None]) & used[None, :]).astype(jnp.float32)
            result = jnp.einsum('bk,kiw->biw', onehot, prod, precision=lax.Precision.HIGHEST).reshape(rows_blk, width)
            start = (rpos * rows_blk).astype(jnp.int32)
        current = lax.dynamic_slice_in_dim(total, start, result.shape[0], 0)
        return lax.dynamic_update_slice_in_dim(total, current + result, start, 0)
    return lax.fori_loop(0, N_ROW * N_COL, visit, jnp.zeros((NORDER, width), jnp.float32))

def reference(blocks, positions, counts, sketch):
    first = spread(blocks, positions, counts, sketch, False).astype(jnp.bfloat16)
    middle = spread(blocks, positions, counts, first, True).astype(jnp.bfloat16)
    power = spread(blocks, positions, counts, middle, False)
    gram = jnp.dot(power.T.astype(jnp.float32), power.astype(jnp.float32), precision=lax.Precision.HIGHEST, preferred_element_type=jnp.float32) / NORDER
    lower = jnp.linalg.cholesky(gram)
    basis = jax.scipy.linalg.solve_triangular(lower, power.T, lower=True).T
    projected = spread(blocks, positions, counts, basis.astype(jnp.bfloat16), True)
    return (basis, projected)
```

```python
import functools

import jax
import jax.numpy as jnp
from jax import lax
from jax.experimental import pallas as pl
from jax.experimental.pallas import tpu as pltpu
from jax.sharding import PartitionSpec as P

MESH = pl.DeviceIdType.MESH
F32 = jnp.float32
BF16 = jnp.bfloat16
DMA = pltpu.SemaphoreType.DMA
HIGHEST = lax.Precision.HIGHEST

NZ = 8
SIDE = 4
CHUNK = 128
WIDTH = 288
HALF = 144
SUB = 96
NSUB = WIDTH // SUB
SLOTS = 96
PACKED = 64


class Place:
    def __init__(self):
        self.r = lax.axis_index("row")
        self.c = lax.axis_index("col")
        self.y = self.c // 8
        self.x = (self.c // 2) % SIDE
        self.k = self.c % 2

    def x_peer(self, i):
        return (self.r, (self.y * SIDE + (self.x + i) % SIDE) * 2 + self.k)

    def y_peer(self, i):
        return (self.r, (((self.y + i) % SIDE) * SIDE + self.x) * 2 + self.k)

    def sibling(self):
        return (self.r, self.c + 1 - 2 * self.k)

    def z_peer(self, i):
        return ((self.r + i) % NZ, self.c)

    def col_peer(self, i):
        return (self.r, (self.c + i) % 32)


def greet(peers):
    barrier = pltpu.get_barrier_semaphore()
    for peer in peers:
        pl.semaphore_signal(barrier, inc=1, device_id=peer, device_id_type=MESH)
    pl.semaphore_wait(barrier, len(peers))


def send(src, dst, send_sem, recv_sem, peer):
    copy = pltpu.make_async_remote_copy(
        src_ref=src,
        dst_ref=dst,
        send_sem=send_sem,
        recv_sem=recv_sem,
        device_id=peer,
        device_id_type=MESH,
    )
    copy.start()
    return copy


def lanes(chunk):
    return pl.ds(pl.multiple_of(chunk * CHUNK, CHUNK), CHUNK)


def gather_z_piece(me, full, sems, piece, pending):
    rows = pl.ds(piece * SUB, SUB)
    send_sem, recv_sem = sems

    def go(step, way):
        owner = (me.r - way * step + NZ) % NZ
        block = full.at[rows, lanes(owner)]
        n = (0 if way == 1 else 4) + step
        copy = send(block, block, send_sem.at[piece, n], recv_sem.at[piece, n], me.z_peer(way % NZ))
        pending.append(copy)
        return copy

    return go


def gather_z(me, full, sems, before=None):
    pending = []
    goes = [gather_z_piece(me, full, sems, piece, pending) for piece in range(NSUB)]
    held = {}
    for step in range(4):
        for piece in range(NSUB):
            if step > 0:
                for copy in held[piece]:
                    copy.wait_recv()
            elif before is not None:
                before(piece)
            copies = [goes[piece](step, 1)]
            if step < 3:
                copies.append(goes[piece](step, -1))
            held[piece] = copies
    for piece in range(NSUB):
        for copy in held[piece]:
            copy.wait_recv()
    return pending


def scatter_z(me, part, up, down, sems, finish):
    send_sem, recv_sem = sems
    pending = []
    held = {}
    for step in range(4):
        for piece in range(NSUB):
            rows = pl.ds(piece * SUB, SUB)
            copies = []
            target = (me.r + 4 + step) % NZ
            if step == 0:
                src = part.at[target, rows]
            else:
                held[piece][0].wait_recv()
                src = up.at[step - 1, rows]
                src[...] += part[target, rows]
            copies.append(
                send(src, up.at[step, rows], send_sem.at[piece, step], recv_sem.at[piece, step], me.z_peer(NZ - 1))
            )
            if step < 3:
                target = (me.r + 3 - step) % NZ
                if step == 0:
                    src = part.at[target, rows]
                else:
                    held[piece][1].wait_recv()
                    src = down.at[step - 1, rows]
                    src[...] += part[target, rows]
                copies.append(
                    send(
                        src, down.at[step, rows], send_sem.at[piece, 4 + step], recv_sem.at[piece, 4 + step], me.z_peer(1)
                    )
                )
            else:
                copies.append(held[piece][1])
            held[piece] = copies
            pending.extend(copies if step < 3 else copies[:1])

    def before(piece):
        rows = pl.ds(piece * SUB, SUB)
        held[piece][0].wait_recv()
        held[piece][1].wait_recv()
        finish(piece, part[me.r, rows] + up[3, rows] + down[2, rows])

    return before, pending


def scatter_col(me, part, other, summed, inbox, inbox2, totals, sems, compute):
    send_sem, recv_sem = sems
    pending = []
    order = [(me.y + i) % SIDE for i in (1, 2, 3, 0)]
    crossing = []
    for i, y in enumerate(order):
        compute(1 - me.k, y)
        crossing.append(send(part.at[1 - me.k, y], other.at[y], send_sem.at[i], recv_sem.at[i], me.sibling()))
    for y in order:
        compute(me.k, y)
    pending.extend(crossing)
    low, high = pl.ds(0, HALF), pl.ds(HALF, HALF)
    first = []
    for i, y in enumerate(order):
        crossing[i].wait_recv()
        for x in range(SIDE):
            summed[y, x] = (part[me.k, y, x] + other[y, x]).astype(summed.dtype)
        if i < 3:
            n = 4 + i
            first.append(
                send(summed.at[y, :, high], inbox.at[1, i], send_sem.at[n], recv_sem.at[n], me.y_peer(i + 1))
            )
    for i in range(3):
        n = 7 + i
        x = (me.x + i + 1) % SIDE
        first.append(send(summed.at[:, x, low], inbox.at[0, i], send_sem.at[n], recv_sem.at[n], me.x_peer(i + 1)))
    for copy in first:
        copy.wait_recv()
    pending.extend(first)
    second = []
    for i in (1, 2, 3, 0):
        y, x = (me.y + i) % SIDE, (me.x + i) % SIDE
        total = summed[y, me.x, low].astype(F32)
        for j in range(3):
            total += inbox[0, j, y].astype(F32)
        totals[0, y] = total.astype(totals.dtype)
        if i:
            n = 9 + i
            second.append(
                send(totals.at[0, y], inbox2.at[0, i - 1], send_sem.at[n], recv_sem.at[n], me.y_peer(i))
            )
        total = summed[me.y, x, high].astype(F32)
        for j in range(3):
            total += inbox[1, j, x].astype(F32)
        totals[1, x] = total.astype(totals.dtype)
        if i:
            n = 12 + i
            second.append(
                send(totals.at[1, x], inbox2.at[1, i - 1], send_sem.at[n], recv_sem.at[n], me.x_peer(i))
            )
    for copy in second:
        copy.wait_recv()
    pending.extend(second)
    halves = []
    for h, mine in enumerate((me.y, me.x)):
        total = totals[h, mine].astype(F32)
        for j in range(3):
            total += inbox2[h, j].astype(F32)
        halves.append(total)
    return halves, pending


def gather_col(me, full, sems):
    send_sem, recv_sem = sems
    pending = []
    k, y, x = me.k, me.y, me.x
    low, high = pl.ds(0, HALF), pl.ds(HALF, HALF)
    first = []
    for i in (1, 2, 3):
        block = full.at[k, y, x, low]
        first.append(send(block, block, send_sem.at[i - 1], recv_sem.at[i - 1], me.y_peer(i)))
        block = full.at[k, y, x, high]
        first.append(send(block, block, send_sem.at[i + 2], recv_sem.at[i + 2], me.x_peer(i)))
    for copy in first:
        copy.wait_recv()
    pending.extend(first)
    second = []
    for i in (1, 2, 3):
        block = full.at[k, :, x, low]
        second.append(send(block, block, send_sem.at[i + 5], recv_sem.at[i + 5], me.x_peer(i)))
        block = full.at[k, y, :, high]
        second.append(send(block, block, send_sem.at[i + 8], recv_sem.at[i + 8], me.y_peer(i)))
    third = []

    def cross(n, block):
        third.append(send(block, block, send_sem.at[n], recv_sem.at[n], me.sibling()))

    cross(12, full.at[k, :, x, low])
    cross(13, full.at[k, y, :, high])
    for i in (1, 3, 2):
        second[2 * i - 2].wait_recv()
        cross(13 + i, full.at[k, :, (x - i + SIDE) % SIDE, low])
        second[2 * i - 1].wait_recv()
        cross(16 + i, full.at[k, (y - i + SIDE) % SIDE, :, high])
    pending.extend(second)
    for copy in third:
        copy.wait_recv()
    pending.extend(third)
    return pending


def dot(a, b, contract, precision=None):
    return lax.dot_general(a, b, ((contract[:1], contract[1:]), ((), ())), precision=precision, preferred_element_type=F32)


def forward(operand, matrix, part):
    def compute(core, y):
        for half in range(2):
            start = pl.multiple_of((core * 16 + y * 4 + half * 2) * CHUNK, 256)
            out = dot(operand[...], matrix[pl.ds(start, 256), :], (1, 1))
            part[core, y, 2 * half] = out[:, :CHUNK]
            part[core, y, 2 * half + 1] = out[:, CHUNK:]

    return compute


def flatten(full, flat):
    def body(n, carry):
        core, y, x = n // 16, (n // 4) % 4, n % 4
        flat[:, pl.ds(pl.multiple_of(n * CHUNK, CHUNK), CHUNK)] = full[core, y, x]
        return carry

    lax.fori_loop(0, 32, body, 0)


def backward(flat, matrix, part):
    def body(n, carry):
        start = pl.multiple_of(n * 256, 256)
        out = dot(flat[...], matrix[:, pl.ds(start, 256)], (1, 0))
        part[2 * n] = out[:, :CHUNK]
        part[2 * n + 1] = out[:, CHUNK:]
        return carry

    lax.fori_loop(0, 4, body, 0)


def packed_tiles():
    return [(g, t) for g in range(36) for t in range((g * 8 + 7) // CHUNK + 1)]


def sample_kernel(
    blocks_ref, slot_ref, sketch_ref, power_ref, gram_ref, matrix_out,
    tiles, matrix, operand, middle, part, other, sum_f, inbox_f, inbox2_f, totals_f,
    sum_h, inbox_h, inbox2_h, totals_h, full, flat, zpart, up, down, gram, packed, gathered, sums, sums_z,
    ga_s, ga_r, gb_s, gb_r, za_s, za_r, ca_s, ca_r, cb_s, cb_r, fa_s, fa_r, g1_s, g1_r, g2_s, g2_r, g3_s, g3_r, local,
):
    me = Place()
    pending = []
    load = pltpu.make_async_copy(blocks_ref, tiles.at[pl.ds(0, SLOTS)], local.at[0])
    load.start()
    greet([me.col_peer(i) for i in range(1, 32)] + [me.z_peer(i) for i in range(1, NZ)])
    operand[:, lanes(me.r)] = sketch_ref[...].astype(F32).T.astype(BF16)
    tiles[SLOTS] = jnp.zeros((CHUNK, CHUNK), BF16)

    load.wait()

    def build(n, carry):
        start = pl.multiple_of(((n % 2) * 16 + n // 2) * CHUNK, CHUNK)
        for t in range(8):
            matrix[pl.ds(start, CHUNK), t * CHUNK : (t + 1) * CHUNK] = tiles[slot_ref[n * 8 + t]]
        return carry

    pending += gather_z(me, operand, (ga_s, ga_r), lambda piece: None)
    lax.fori_loop(0, 32, build, 0)
    keep = pltpu.make_async_copy(matrix, matrix_out, local.at[1])
    keep.start()

    halves, more = scatter_col(
        me, part, other, sum_f, inbox_f, inbox2_f, totals_f, (ca_s, ca_r), forward(operand, matrix, part)
    )
    for copy in more:
        copy.wait_send()
    full[me.k, me.y, me.x, pl.ds(0, HALF)] = halves[0].astype(BF16)
    full[me.k, me.y, me.x, pl.ds(HALF, HALF)] = halves[1].astype(BF16)
    pending += gather_col(me, full, (fa_s, fa_r))
    flatten(full, flat)
    backward(flat, matrix, zpart)

    def finish(piece, total):
        middle[pl.ds(piece * SUB, SUB), lanes(me.r)] = total.astype(BF16)

    before, more = scatter_z(me, zpart, up, down, (za_s, za_r), finish)
    pending += more
    pending += gather_z(me, middle, (gb_s, gb_r), before)

    halves, more = scatter_col(
        me, part, other, sum_h, inbox_h, inbox2_h, totals_h, (cb_s, cb_r), forward(middle, matrix, part)
    )
    pending += more
    power_ref[pl.ds(0, HALF)] = halves[0]
    power_ref[pl.ds(HALF, HALF)] = halves[1]

    gram[...] = jnp.zeros_like(gram)
    gram[:, 0:WIDTH] = dot(power_ref[...], power_ref[...], (1, 1), HIGHEST)
    for n, (g, t) in enumerate(packed_tiles()):
        packed[n] = gram[g * 8 : g * 8 + 8, t * CHUNK : (t + 1) * CHUNK]
    for n in range(len(packed_tiles()), PACKED):
        packed[n] = jnp.zeros((8, CHUNK), F32)
    copies = []
    for i in range(1, 32):
        copies.append(
            send(packed.at[pl.ds(2 * ((me.c + i) % 32), 2)], gathered.at[me.c], g1_s.at[i], g1_r.at[i], me.col_peer(i))
        )
    for copy in copies:
        copy.wait_recv()
    pending += copies
    gathered[me.c] = packed[pl.ds(2 * me.c, 2)]
    total = gathered[0]
    for i in range(1, 32):
        total += gathered[i]
    sums_z[me.r] = total
    copies = []
    for i in (4, 3, 5, 2, 6, 1, 7):
        copies.append(send(sums_z.at[me.r], sums_z.at[me.r], g2_s.at[i], g2_r.at[i], me.z_peer(i)))
    for copy in copies:
        copy.wait_recv()
    pending += copies
    total = sums_z[0]
    for i in range(1, NZ):
        total += sums_z[i]
    sums[me.c] = total
    copies = []
    for i in range(1, 32):
        copies.append(send(sums.at[me.c], sums.at[me.c], g3_s.at[i], g3_r.at[i], me.col_peer(i)))
    for copy in copies:
        copy.wait_recv()
    pending += copies
    for n in range(32):
        gram_ref[2 * n] = sums[n, 0]
        gram_ref[2 * n + 1] = sums[n, 1]
    for copy in pending:
        copy.wait_send()
    keep.wait()


def basis_kernel(gram_ref, power_ref, basis_ref, low_ref, work):
    work[WIDTH:] = jnp.zeros((384 - WIDTH, 512), F32)
    for n, (g, t) in enumerate(packed_tiles()):
        work[g * 8 : g * 8 + 8, t * CHUNK : (t + 1) * CHUNK] = gram_ref[n] * (1.0 / 32768.0)
    work[0:128, 128:256] = work[128:256, 0:128].T
    work[0:128, 256:384] = work[256:384, 0:128].T
    work[128:256, 256:384] = work[256:384, 128:256].T
    work[0:WIDTH, 384:512] = power_ref[...]
    row = lax.broadcasted_iota(jnp.int32, (32, CHUNK), 0)
    lane = lax.broadcasted_iota(jnp.int32, (32, CHUNK), 1)
    for panel in range(9):
        r0 = panel * 32
        tile, off = r0 // CHUNK, r0 % CHUNK
        left = work[r0 : r0 + 32, tile * CHUNK : (tile + 1) * CHUNK]
        right = (lane == row + off).astype(F32)
        for j in range(32):
            col = left[:, off + j : off + j + 1]
            scale = lax.rsqrt(col[j : j + 1])
            pick = row == j
            factor = jnp.where(row > j, col * scale, 0.0)
            left_row = left[j : j + 1] * scale
            right_row = right[j : j + 1] * scale
            left = jnp.where(pick, left_row, left - factor * left_row)
            right = jnp.where(pick, right_row, right - factor * right_row)
        block = pl.ds(tile * CHUNK, CHUNK)
        upper = dot(right, work[block, :], (1, 0), HIGHEST)
        if panel < 8:
            below = work[r0 + 32 : WIDTH, tile * CHUNK : (tile + 1) * CHUNK]
            lower = dot(below, right, (1, 1), HIGHEST)
            work[r0 + 32 : WIDTH, :] -= dot(lower, upper, (1, 0), HIGHEST)
        solved = upper[:, 384:512]
        low_ref[r0 : r0 + 32] = solved.astype(BF16)
        work[r0 : r0 + 32, 384:512] = solved
    basis_ref[...] = work[0:WIDTH, 384:512].T


def project_kernel(
    low_ref, matrix_in, out_ref, matrix, full, flat, zpart, up, down, fa_s, fa_r, za_s, za_r, local
):
    me = Place()
    load = pltpu.make_async_copy(matrix_in, matrix, local.at[0])
    load.start()
    greet(
        [me.x_peer(i) for i in (1, 2, 3)]
        + [me.y_peer(i) for i in (1, 2, 3)]
        + [me.sibling(), me.z_peer(1), me.z_peer(NZ - 1)]
    )
    full[me.k, me.y, me.x] = low_ref[...]
    pending = gather_col(me, full, (fa_s, fa_r))
    flatten(full, flat)
    load.wait()
    backward(flat, matrix, zpart)

    def finish(piece, total):
        out_ref[:, piece * SUB : (piece + 1) * SUB] = total.T

    before, more = scatter_z(me, zpart, up, down, (za_s, za_r), finish)
    for piece in range(NSUB):
        before(piece)
    for copy in pending + more:
        copy.wait_send()


def sem(*shape):
    return [DMA(shape), DMA(shape)]


def local(blocks, positions, counts, sketch):
    places = positions[0, 0]
    used = lax.iota(jnp.int32, SLOTS) < counts[0, 0]
    where = jnp.where(used, places, -1)
    hit = where[None, :] == lax.iota(jnp.int32, 256)[:, None]
    slots = jnp.min(jnp.where(hit, lax.iota(jnp.int32, SLOTS)[None, :], SLOTS), axis=1)

    vmem = pl.BlockSpec(memory_space=pltpu.VMEM)
    hbm = pl.BlockSpec(memory_space=pl.ANY)
    smem = pl.BlockSpec(memory_space=pltpu.SMEM)
    V = pltpu.VMEM
    power, gram, matrix = pl.pallas_call(
        sample_kernel,
        out_shape=[
            jax.ShapeDtypeStruct((WIDTH, CHUNK), F32),
            jax.ShapeDtypeStruct((PACKED, 8, CHUNK), F32),
            jax.ShapeDtypeStruct((4096, 1024), BF16),
        ],
        in_specs=[hbm, smem, vmem],
        out_specs=[vmem, vmem, hbm],
        scratch_shapes=[
            V((SLOTS + 1, CHUNK, CHUNK), BF16),
            V((4096, 1024), BF16),
            V((WIDTH, 1024), BF16),
            V((WIDTH, 1024), BF16),
            V((2, SIDE, SIDE, WIDTH, CHUNK), F32),
            V((SIDE, SIDE, WIDTH, CHUNK), F32),
            V((SIDE, SIDE, WIDTH, CHUNK), F32),
            V((2, 3, SIDE, HALF, CHUNK), F32),
            V((2, 3, HALF, CHUNK), F32),
            V((2, SIDE, HALF, CHUNK), F32),
            V((SIDE, SIDE, WIDTH, CHUNK), BF16),
            V((2, 3, SIDE, HALF, CHUNK), BF16),
            V((2, 3, HALF, CHUNK), BF16),
            V((2, SIDE, HALF, CHUNK), BF16),
            V((2, SIDE, SIDE, WIDTH, CHUNK), BF16),
            V((WIDTH, 4096), BF16),
            V((NZ, WIDTH, CHUNK), F32),
            V((4, WIDTH, CHUNK), F32),
            V((3, WIDTH, CHUNK), F32),
            V((WIDTH, 384), F32),
            V((PACKED, 8, CHUNK), F32),
            V((32, 2, 8, CHUNK), F32),
            V((32, 2, 8, CHUNK), F32),
            V((NZ, 2, 8, CHUNK), F32),
            *sem(NSUB, 7),
            *sem(NSUB, 7),
            *sem(NSUB, 7),
            *sem(16),
            *sem(16),
            *sem(20),
            *sem(32),
            *sem(8),
            *sem(32),
            DMA((2,)),
        ],
        compiler_params=pltpu.CompilerParams(
            collective_id=1, has_side_effects=True, vmem_limit_bytes=56 << 20
        ),
    )(blocks[0, 0], slots, sketch)

    basis, low = pl.pallas_call(
        basis_kernel,
        out_shape=[jax.ShapeDtypeStruct((CHUNK, WIDTH), F32), jax.ShapeDtypeStruct((WIDTH, CHUNK), BF16)],
        in_specs=[vmem, vmem],
        out_specs=[vmem, vmem],
        scratch_shapes=[V((384, 512), F32)],
        compiler_params=pltpu.CompilerParams(vmem_limit_bytes=40 << 20),
    )(gram, power)

    projected = pl.pallas_call(
        project_kernel,
        out_shape=jax.ShapeDtypeStruct((CHUNK, WIDTH), F32),
        in_specs=[vmem, hbm],
        out_specs=vmem,
        scratch_shapes=[
            V((4096, 1024), BF16),
            V((2, SIDE, SIDE, WIDTH, CHUNK), BF16),
            V((WIDTH, 4096), BF16),
            V((NZ, WIDTH, CHUNK), F32),
            V((4, WIDTH, CHUNK), F32),
            V((3, WIDTH, CHUNK), F32),
            *sem(20),
            *sem(NSUB, 7),
            DMA((1,)),
        ],
        compiler_params=pltpu.CompilerParams(
            collective_id=2, has_side_effects=True, vmem_limit_bytes=56 << 20
        ),
    )(low, matrix)
    return (basis, projected)


def solution(mesh):
    return jax.shard_map(
        local,
        mesh=mesh,
        in_specs=(
            P("row", "col", None, None, None),
            P("row", "col", None),
            P("row", "col"),
            P(("col", "row"), None),
        ),
        out_specs=(P(("row", "col"), None), P(("col", "row"), None)),
        check_vma=False,
    )
```

```python
import functools

import jax
import jax.numpy as jnp
from jax import lax
from jax.experimental import pallas as pl
from jax.experimental.pallas import tpu as pltpu
from jax.sharding import PartitionSpec as P

MESH = pl.DeviceIdType.MESH
F32 = jnp.float32
BF16 = jnp.bfloat16
DMA = pltpu.SemaphoreType.DMA
HIGHEST = lax.Precision.HIGHEST

NZ = 8
SIDE = 4
CHUNK = 128
WIDTH = 288
HALF = 144
SUB = 96
NSUB = WIDTH // SUB
SLOTS = 96
PACKED = 64


class Place:
    def __init__(self):
        self.r = lax.axis_index("row")
        self.c = lax.axis_index("col")
        self.y = self.c // 8
        self.x = (self.c // 2) % SIDE
        self.k = self.c % 2

    def x_peer(self, i):
        return (self.r, (self.y * SIDE + (self.x + i) % SIDE) * 2 + self.k)

    def y_peer(self, i):
        return (self.r, (((self.y + i) % SIDE) * SIDE + self.x) * 2 + self.k)

    def sibling(self):
        return (self.r, self.c + 1 - 2 * self.k)

    def z_peer(self, i):
        return ((self.r + i) % NZ, self.c)

    def col_peer(self, i):
        return (self.r, (self.c + i) % 32)


def greet(peers):
    barrier = pltpu.get_barrier_semaphore()
    for peer in peers:
        pl.semaphore_signal(barrier, inc=1, device_id=peer, device_id_type=MESH)
    pl.semaphore_wait(barrier, len(peers))


def send(src, dst, send_sem, recv_sem, peer):
    copy = pltpu.make_async_remote_copy(
        src_ref=src,
        dst_ref=dst,
        send_sem=send_sem,
        recv_sem=recv_sem,
        device_id=peer,
        device_id_type=MESH,
    )
    copy.start()
    return copy


def lanes(chunk):
    return pl.ds(pl.multiple_of(chunk * CHUNK, CHUNK), CHUNK)


def gather_z_piece(me, full, sems, piece, pending):
    rows = pl.ds(piece * SUB, SUB)
    send_sem, recv_sem = sems

    def go(step, way):
        owner = (me.r - way * step + NZ) % NZ
        block = full.at[rows, lanes(owner)]
        n = (0 if way == 1 else 4) + step
        copy = send(block, block, send_sem.at[piece, n], recv_sem.at[piece, n], me.z_peer(way % NZ))
        pending.append(copy)
        return copy

    return go


def gather_z(me, full, sems, before, meanwhile=None):
    pending = []
    goes = [gather_z_piece(me, full, sems, piece, pending) for piece in range(NSUB)]
    held = {}
    for step in range(4):
        for piece in range(NSUB):
            if step > 0:
                for copy in held[piece]:
                    copy.wait_recv()
            else:
                before(piece)
            copies = [goes[piece](step, 1)]
            if step < 3:
                copies.append(goes[piece](step, -1))
            held[piece] = copies
        if step == 0 and meanwhile is not None:
            meanwhile()
    for piece in range(NSUB):
        for copy in held[piece]:
            copy.wait_recv()
    return pending


def scatter_z(me, part, up, down, sems, finish):
    send_sem, recv_sem = sems
    pending = []
    held = {}
    for step in range(4):
        for piece in range(NSUB):
            rows = pl.ds(piece * SUB, SUB)
            copies = []
            target = (me.r + 4 + step) % NZ
            if step == 0:
                src = part.at[target, rows]
            else:
                held[piece][0].wait_recv()
                src = up.at[step - 1, rows]
                src[...] += part[target, rows]
            copies.append(
                send(src, up.at[step, rows], send_sem.at[piece, step], recv_sem.at[piece, step], me.z_peer(NZ - 1))
            )
            if step < 3:
                target = (me.r + 3 - step) % NZ
                if step == 0:
                    src = part.at[target, rows]
                else:
                    held[piece][1].wait_recv()
                    src = down.at[step - 1, rows]
                    src[...] += part[target, rows]
                copies.append(
                    send(
                        src, down.at[step, rows], send_sem.at[piece, 4 + step], recv_sem.at[piece, 4 + step], me.z_peer(1)
                    )
                )
            else:
                copies.append(held[piece][1])
            held[piece] = copies
            pending.extend(copies if step < 3 else copies[:1])

    def before(piece):
        rows = pl.ds(piece * SUB, SUB)
        held[piece][0].wait_recv()
        held[piece][1].wait_recv()
        finish(piece, part[me.r, rows] + up[3, rows] + down[2, rows])

    return before, pending


def scatter_col(me, part, other, summed, inbox, inbox2, totals, sems, compute):
    send_sem, recv_sem = sems
    pending = []
    order = [(me.y + i) % SIDE for i in (1, 2, 3, 0)]
    crossing = []
    for i, y in enumerate(order):
        compute(1 - me.k, y)
        crossing.append(send(part.at[1 - me.k, y], other.at[y], send_sem.at[i], recv_sem.at[i], me.sibling()))
    for y in order:
        compute(me.k, y)
    pending.extend(crossing)
    low, high = pl.ds(0, HALF), pl.ds(HALF, HALF)
    first = []
    for i, y in enumerate(order):
        crossing[i].wait_recv()
        for x in range(SIDE):
            summed[y, x] = (part[me.k, y, x] + other[y, x]).astype(summed.dtype)
        if i < 3:
            n = 4 + i
            first.append(
                send(summed.at[y, :, high], inbox.at[1, i], send_sem.at[n], recv_sem.at[n], me.y_peer(i + 1))
            )
    for i in range(3):
        n = 7 + i
        x = (me.x + i + 1) % SIDE
        first.append(send(summed.at[:, x, low], inbox.at[0, i], send_sem.at[n], recv_sem.at[n], me.x_peer(i + 1)))
    for copy in first:
        copy.wait_recv()
    pending.extend(first)
    second = []
    for i in (1, 2, 3, 0):
        y, x = (me.y + i) % SIDE, (me.x + i) % SIDE
        total = summed[y, me.x, low].astype(F32)
        for j in range(3):
            total += inbox[0, j, y].astype(F32)
        totals[0, y] = total.astype(totals.dtype)
        if i:
            n = 9 + i
            second.append(
                send(totals.at[0, y], inbox2.at[0, i - 1], send_sem.at[n], recv_sem.at[n], me.y_peer(i))
            )
        total = summed[me.y, x, high].astype(F32)
        for j in range(3):
            total += inbox[1, j, x].astype(F32)
        totals[1, x] = total.astype(totals.dtype)
        if i:
            n = 12 + i
            second.append(
                send(totals.at[1, x], inbox2.at[1, i - 1], send_sem.at[n], recv_sem.at[n], me.x_peer(i))
            )
    for copy in second:
        copy.wait_recv()
    pending.extend(second)
    halves = []
    for h, mine in enumerate((me.y, me.x)):
        total = totals[h, mine].astype(F32)
        for j in range(3):
            total += inbox2[h, j].astype(F32)
        halves.append(total)
    return halves, pending


def gather_col(me, full, sems, between=(lambda: None, lambda: None, lambda: None)):
    send_sem, recv_sem = sems
    pending = []
    k, y, x = me.k, me.y, me.x
    low, high = pl.ds(0, HALF), pl.ds(HALF, HALF)
    first = []
    for i in (1, 2, 3):
        block = full.at[k, y, x, low]
        first.append(send(block, block, send_sem.at[i - 1], recv_sem.at[i - 1], me.y_peer(i)))
        block = full.at[k, y, x, high]
        first.append(send(block, block, send_sem.at[i + 2], recv_sem.at[i + 2], me.x_peer(i)))
    between[0]()
    for copy in first:
        copy.wait_recv()
    pending.extend(first)
    second = []
    for i in (1, 2, 3):
        block = full.at[k, :, x, low]
        second.append(send(block, block, send_sem.at[i + 5], recv_sem.at[i + 5], me.x_peer(i)))
        block = full.at[k, y, :, high]
        second.append(send(block, block, send_sem.at[i + 8], recv_sem.at[i + 8], me.y_peer(i)))
    third = []

    def cross(n, block):
        third.append(send(block, block, send_sem.at[n], recv_sem.at[n], me.sibling()))

    cross(12, full.at[k, :, x, low])
    cross(13, full.at[k, y, :, high])
    between[1]()
    for i in (1, 3, 2):
        second[2 * i - 2].wait_recv()
        cross(13 + i, full.at[k, :, (x - i + SIDE) % SIDE, low])
        second[2 * i - 1].wait_recv()
        cross(16 + i, full.at[k, (y - i + SIDE) % SIDE, :, high])
    pending.extend(second)
    between[2]()
    for copy in third:
        copy.wait_recv()
    pending.extend(third)
    return pending


def dot(a, b, contract, precision=None):
    return lax.dot_general(a, b, ((contract[:1], contract[1:]), ((), ())), precision=precision, preferred_element_type=F32)


def forward(operand, matrix, part):
    def compute(core, y):
        for half in range(2):
            start = pl.multiple_of((core * 16 + y * 4 + half * 2) * CHUNK, 256)
            out = dot(operand[...], matrix[pl.ds(start, 256), :], (1, 1))
            part[core, y, 2 * half] = out[:, :CHUNK]
            part[core, y, 2 * half + 1] = out[:, CHUNK:]

    return compute


def flatten(full, flat):
    def body(n, carry):
        core, y, x = n // 16, (n // 4) % 4, n % 4
        flat[:, pl.ds(pl.multiple_of(n * CHUNK, CHUNK), CHUNK)] = full[core, y, x]
        return carry

    lax.fori_loop(0, 32, body, 0)


def backward(flat, matrix, part):
    def body(n, carry):
        start = pl.multiple_of(n * 256, 256)
        out = dot(flat[...], matrix[:, pl.ds(start, 256)], (1, 0))
        part[2 * n] = out[:, :CHUNK]
        part[2 * n + 1] = out[:, CHUNK:]
        return carry

    lax.fori_loop(0, 4, body, 0)


def packed_tiles():
    return [(g, t) for g in range(36) for t in range((g * 8 + 7) // CHUNK + 1)]


def sample_kernel(
    blocks_ref, slot_ref, sketch_ref, power_ref, second_ref, gram_ref,
    tiles, matrix, operand, middle, part, other, sum_f, inbox_f, inbox2_f, totals_f,
    sum_h, inbox_h, inbox2_h, totals_h, full, full2, flat, zpart, up, down, up2, down2, gram, packed, gathered, sums, sums_z,
    ga_s, ga_r, gb_s, gb_r, za_s, za_r, zb_s, zb_r, ca_s, ca_r, cb_s, cb_r, fa_s, fa_r, fb_s, fb_r,
    g1_s, g1_r, g2_s, g2_r, g3_s, g3_r, local,
):
    me = Place()
    pending = []
    load = pltpu.make_async_copy(blocks_ref, tiles.at[pl.ds(0, SLOTS)], local.at[0])
    load.start()
    operand[:, lanes(me.r)] = sketch_ref[...]
    tiles[SLOTS] = jnp.zeros((CHUNK, CHUNK), BF16)
    greet([me.col_peer(i) for i in range(1, 32)] + [me.z_peer(i) for i in range(1, NZ)])

    def build(n, carry):
        start = pl.multiple_of(((n % 2) * 16 + n // 2) * CHUNK, CHUNK)
        for t in range(8):
            matrix[pl.ds(start, CHUNK), t * CHUNK : (t + 1) * CHUNK] = tiles[slot_ref[n * 8 + t]]
        return carry

    def build_all():
        load.wait()
        lax.fori_loop(0, 32, build, 0)

    pending += gather_z(me, operand, (ga_s, ga_r), lambda piece: None, build_all)

    halves, more = scatter_col(
        me, part, other, sum_f, inbox_f, inbox2_f, totals_f, (ca_s, ca_r), forward(operand, matrix, part)
    )
    for copy in more:
        copy.wait_send()
    full[me.k, me.y, me.x, pl.ds(0, HALF)] = halves[0].astype(BF16)
    full[me.k, me.y, me.x, pl.ds(HALF, HALF)] = halves[1].astype(BF16)
    pending += gather_col(me, full, (fa_s, fa_r))
    flatten(full, flat)
    backward(flat, matrix, zpart)

    def finish(piece, total):
        middle[pl.ds(piece * SUB, SUB), lanes(me.r)] = total.astype(BF16)

    before, more = scatter_z(me, zpart, up, down, (za_s, za_r), finish)
    pending += gather_z(me, middle, (gb_s, gb_r), before)
    for copy in more:
        copy.wait_send()

    halves, more = scatter_col(
        me, part, other, sum_h, inbox_h, inbox2_h, totals_h, (cb_s, cb_r), forward(middle, matrix, part)
    )
    pending += more
    power_ref[pl.ds(0, HALF)] = halves[0]
    power_ref[pl.ds(HALF, HALF)] = halves[1]
    full2[me.k, me.y, me.x, pl.ds(0, HALF)] = halves[0].astype(BF16)
    full2[me.k, me.y, me.x, pl.ds(HALF, HALF)] = halves[1].astype(BF16)

    sent = []

    def gram_part():
        gram[...] = jnp.zeros_like(gram)
        gram[:, 0:WIDTH] = dot(power_ref[...], power_ref[...], (1, 1), HIGHEST)
        for n, (g, t) in enumerate(packed_tiles()):
            packed[n] = gram[g * 8 : g * 8 + 8, t * CHUNK : (t + 1) * CHUNK]
        for n in range(len(packed_tiles()), PACKED):
            packed[n] = jnp.zeros((8, CHUNK), F32)
        for i in range(1, 32):
            sent.append(
                send(packed.at[pl.ds(2 * ((me.c + i) % 32), 2)], gathered.at[me.c], g1_s.at[i], g1_r.at[i], me.col_peer(i))
            )

    def gram_col():
        for copy in sent:
            copy.wait_recv()
        gathered[me.c] = packed[pl.ds(2 * me.c, 2)]
        total = gathered[0]
        for i in range(1, 32):
            total += gathered[i]
        sums_z[me.r] = total
        pending.extend(sent)
        sent.clear()
        for i in (4, 3, 5, 2, 6, 1, 7):
            sent.append(send(sums_z.at[me.r], sums_z.at[me.r], g2_s.at[i], g2_r.at[i], me.z_peer(i)))

    def gram_row():
        for copy in sent:
            copy.wait_recv()
        total = sums_z[0]
        for i in range(1, NZ):
            total += sums_z[i]
        sums[me.c] = total
        pending.extend(sent)
        sent.clear()
        for i in range(1, 32):
            sent.append(send(sums.at[me.c], sums.at[me.c], g3_s.at[i], g3_r.at[i], me.col_peer(i)))

    pending += gather_col(me, full2, (fb_s, fb_r), (gram_part, gram_col, gram_row))
    pending.extend(sent)
    flatten(full2, flat)
    backward(flat, matrix, zpart)

    def keep(piece, total):
        second_ref[piece * SUB : (piece + 1) * SUB] = total

    before, more = scatter_z(me, zpart, up2, down2, (zb_s, zb_r), keep)
    pending += more
    for copy in sent:
        copy.wait_recv()
    for n in range(32):
        gram_ref[2 * n] = sums[n, 0]
        gram_ref[2 * n + 1] = sums[n, 1]
    for piece in range(NSUB):
        before(piece)
    for copy in pending:
        copy.wait_send()


def over_lanes(block, lane):
    return jnp.broadcast_to(block[:, lane : lane + 1], (8, CHUNK))


def over_rows(block, row):
    return jnp.broadcast_to(block[row : row + 1, :], (8, CHUNK))


def invert_factor(left, off):
    row = lax.broadcasted_iota(jnp.int32, (8, CHUNK), 0)
    lane = lax.broadcasted_iota(jnp.int32, (8, CHUNK), 1)
    L = [left[8 * h : 8 * h + 8] for h in range(4)]
    R = [(lane == row + 8 * h + off).astype(F32) for h in range(4)]
    for g in range(4):
        cols = {h: [over_lanes(L[h], off + 8 * g + b) for b in range(8)] for h in range(g, 4)}
        p = [[over_rows(cols[g][b], a) for b in range(a + 1)] for a in range(8)]
        left_rows = [over_rows(L[g], a) for a in range(8)]
        right_rows = [over_rows(R[g], a) for a in range(8)]
        for b in range(8):
            inv = lax.rsqrt(p[b][b])
            for a in range(b + 1, 8):
                p[a][b] = p[a][b] * inv
            for a in range(b + 1, 8):
                for c in range(b + 1, a + 1):
                    p[a][c] = p[a][c] - p[a][b] * p[c][b]
            left_rows[b] = left_rows[b] * inv
            right_rows[b] = right_rows[b] * inv
            for a in range(b + 1, 8):
                left_rows[a] = left_rows[a] - p[a][b] * left_rows[b]
                right_rows[a] = right_rows[a] - p[a][b] * right_rows[b]
            for h in range(g + 1, 4):
                cols[h][b] = cols[h][b] * inv
                for a in range(b + 1, 8):
                    cols[h][a] = cols[h][a] - p[a][b] * cols[h][b]
        for h in range(g + 1, 4):
            for b in range(8):
                L[h] = L[h] - cols[h][b] * left_rows[b]
                R[h] = R[h] - cols[h][b] * right_rows[b]
        new = right_rows[0]
        for a in range(1, 8):
            new = jnp.where(row == a, right_rows[a], new)
        R[g] = new
    return jnp.concatenate(R, 0)


def basis_kernel(gram_ref, power_ref, second_ref, basis_ref, projected_ref, work):
    work[WIDTH:] = jnp.zeros((384 - WIDTH, 640), F32)
    for n, (g, t) in enumerate(packed_tiles()):
        work[g * 8 : g * 8 + 8, t * CHUNK : (t + 1) * CHUNK] = gram_ref[n] * (1.0 / 32768.0)
    work[0:128, 128:256] = work[128:256, 0:128].T
    work[0:128, 256:384] = work[256:384, 0:128].T
    work[128:256, 256:384] = work[256:384, 128:256].T
    work[0:WIDTH, 384:512] = power_ref[...]
    work[0:WIDTH, 512:640] = second_ref[...]
    for panel in range(9):
        r0 = panel * 32
        tile, off = r0 // CHUNK, r0 % CHUNK
        right = invert_factor(work[r0 : r0 + 32, tile * CHUNK : (tile + 1) * CHUNK], off)
        upper = dot(right, work[tile * CHUNK : (tile + 1) * CHUNK, tile * CHUNK :], (1, 0), HIGHEST)
        if panel < 8:
            below = work[r0 + 32 : WIDTH, tile * CHUNK : (tile + 1) * CHUNK]
            lower = dot(below, right, (1, 1), HIGHEST)
            work[r0 + 32 : WIDTH, tile * CHUNK :] -= dot(lower, upper, (1, 0), HIGHEST)
        basis_ref[r0 : r0 + 32] = upper[:, -256:-128]
        projected_ref[r0 : r0 + 32] = upper[:, -128:]


def sem(*shape):
    return [DMA(shape), DMA(shape)]


def local(blocks, positions, counts, sketch):
    places = positions[0, 0]
    used = lax.iota(jnp.int32, SLOTS) < counts[0, 0]
    where = jnp.where(used, places, -1)
    hit = where[None, :] == lax.iota(jnp.int32, 256)[:, None]
    slots = jnp.min(jnp.where(hit, lax.iota(jnp.int32, SLOTS)[None, :], SLOTS), axis=1)

    vmem = pl.BlockSpec(memory_space=pltpu.VMEM)
    hbm = pl.BlockSpec(memory_space=pl.ANY)
    smem = pl.BlockSpec(memory_space=pltpu.SMEM)
    V = pltpu.VMEM
    power, second, gram = pl.pallas_call(
        sample_kernel,
        out_shape=[
            jax.ShapeDtypeStruct((WIDTH, CHUNK), F32),
            jax.ShapeDtypeStruct((WIDTH, CHUNK), F32),
            jax.ShapeDtypeStruct((PACKED, 8, CHUNK), F32),
        ],
        in_specs=[hbm, smem, vmem],
        out_specs=[vmem, vmem, vmem],
        scratch_shapes=[
            V((SLOTS + 1, CHUNK, CHUNK), BF16),
            V((4096, 1024), BF16),
            V((WIDTH, 1024), BF16),
            V((WIDTH, 1024), BF16),
            V((2, SIDE, SIDE, WIDTH, CHUNK), F32),
            V((SIDE, SIDE, WIDTH, CHUNK), F32),
            V((SIDE, SIDE, WIDTH, CHUNK), F32),
            V((2, 3, SIDE, HALF, CHUNK), F32),
            V((2, 3, HALF, CHUNK), F32),
            V((2, SIDE, HALF, CHUNK), F32),
            V((SIDE, SIDE, WIDTH, CHUNK), BF16),
            V((2, 3, SIDE, HALF, CHUNK), BF16),
            V((2, 3, HALF, CHUNK), BF16),
            V((2, SIDE, HALF, CHUNK), BF16),
            V((2, SIDE, SIDE, WIDTH, CHUNK), BF16),
            V((2, SIDE, SIDE, WIDTH, CHUNK), BF16),
            V((WIDTH, 4096), BF16),
            V((NZ, WIDTH, CHUNK), F32),
            V((4, WIDTH, CHUNK), F32),
            V((3, WIDTH, CHUNK), F32),
            V((4, WIDTH, CHUNK), F32),
            V((3, WIDTH, CHUNK), F32),
            V((WIDTH, 384), F32),
            V((PACKED, 8, CHUNK), F32),
            V((32, 2, 8, CHUNK), F32),
            V((32, 2, 8, CHUNK), F32),
            V((NZ, 2, 8, CHUNK), F32),
            *sem(NSUB, 7),
            *sem(NSUB, 7),
            *sem(NSUB, 7),
            *sem(NSUB, 7),
            *sem(16),
            *sem(16),
            *sem(20),
            *sem(20),
            *sem(32),
            *sem(8),
            *sem(32),
            DMA((1,)),
        ],
        compiler_params=pltpu.CompilerParams(
            collective_id=1, has_side_effects=True, vmem_limit_bytes=56 << 20
        ),
    )(blocks[0, 0], slots, sketch.T)

    basis, projected = pl.pallas_call(
        basis_kernel,
        out_shape=[jax.ShapeDtypeStruct((WIDTH, CHUNK), F32)] * 2,
        in_specs=[vmem] * 3,
        out_specs=[vmem] * 2,
        scratch_shapes=[V((384, 640), F32)],
        compiler_params=pltpu.CompilerParams(vmem_limit_bytes=40 << 20),
    )(gram, power, second)
    return (basis.T, projected.T)


def solution(mesh):
    return jax.shard_map(
        local,
        mesh=mesh,
        in_specs=(
            P("row", "col", None, None, None),
            P("row", "col", None),
            P("row", "col"),
            P(("col", "row"), None),
        ),
        out_specs=(P(("row", "col"), None), P(("col", "row"), None)),
        check_vma=False,
    )
```

```python
import functools

import jax
import jax.numpy as jnp
from jax import lax
from jax.experimental import pallas as pl
from jax.experimental.pallas import tpu as pltpu
from jax.sharding import PartitionSpec as P

MESH = pl.DeviceIdType.MESH
F32 = jnp.float32
BF16 = jnp.bfloat16
DMA = pltpu.SemaphoreType.DMA
HIGHEST = lax.Precision.HIGHEST

NZ = 8
SIDE = 4
CHUNK = 128
WIDTH = 288
HALF = 144
SUB = 96
NSUB = WIDTH // SUB
SLOTS = 96
PACKED = 64


class Place:
    def __init__(self):
        self.r = lax.axis_index("row")
        self.c = lax.axis_index("col")
        self.y = self.c // 8
        self.x = (self.c // 2) % SIDE
        self.k = self.c % 2

    def x_peer(self, i):
        return (self.r, (self.y * SIDE + (self.x + i) % SIDE) * 2 + self.k)

    def y_peer(self, i):
        return (self.r, (((self.y + i) % SIDE) * SIDE + self.x) * 2 + self.k)

    def sibling(self):
        return (self.r, self.c + 1 - 2 * self.k)

    def z_peer(self, i):
        return ((self.r + i) % NZ, self.c)

    def col_peer(self, i):
        return (self.r, (self.c + i) % 32)


def greet(peers):
    barrier = pltpu.get_barrier_semaphore()
    for peer in peers:
        pl.semaphore_signal(barrier, inc=1, device_id=peer, device_id_type=MESH)
    pl.semaphore_wait(barrier, len(peers))


def send(src, dst, send_sem, recv_sem, peer):
    copy = pltpu.make_async_remote_copy(
        src_ref=src,
        dst_ref=dst,
        send_sem=send_sem,
        recv_sem=recv_sem,
        device_id=peer,
        device_id_type=MESH,
    )
    copy.start()
    return copy


def lanes(chunk):
    return pl.ds(pl.multiple_of(chunk * CHUNK, CHUNK), CHUNK)


def gather_z_piece(me, full, sems, piece, pending):
    rows = pl.ds(piece * SUB, SUB)
    send_sem, recv_sem = sems

    def go(step, way):
        owner = (me.r - way * step + NZ) % NZ
        block = full.at[rows, lanes(owner)]
        n = (0 if way == 1 else 4) + step
        copy = send(block, block, send_sem.at[piece, n], recv_sem.at[piece, n], me.z_peer(way % NZ))
        pending.append(copy)
        return copy

    return go


def gather_z(me, full, sems, before, meanwhile=None):
    pending = []
    goes = [gather_z_piece(me, full, sems, piece, pending) for piece in range(NSUB)]
    held = {}
    for step in range(4):
        for piece in range(NSUB):
            if step > 0:
                for copy in held[piece]:
                    copy.wait_recv()
            else:
                before(piece)
            copies = [goes[piece](step, 1)]
            if step < 3:
                copies.append(goes[piece](step, -1))
            held[piece] = copies
        if step == 0 and meanwhile is not None:
            meanwhile()
    for piece in range(NSUB):
        for copy in held[piece]:
            copy.wait_recv()
    return pending


def scatter_z(me, part, up, down, sems, finish, between=lambda step: None):
    send_sem, recv_sem = sems
    pending = []
    held = {}
    for step in range(4):
        for piece in range(NSUB):
            rows = pl.ds(piece * SUB, SUB)
            copies = []
            target = (me.r + 4 + step) % NZ
            if step == 0:
                src = part.at[target, rows]
            else:
                held[piece][0].wait_recv()
                src = up.at[step - 1, rows]
                src[...] += part[target, rows]
            copies.append(
                send(src, up.at[step, rows], send_sem.at[piece, step], recv_sem.at[piece, step], me.z_peer(NZ - 1))
            )
            if step < 3:
                target = (me.r + 3 - step) % NZ
                if step == 0:
                    src = part.at[target, rows]
                else:
                    held[piece][1].wait_recv()
                    src = down.at[step - 1, rows]
                    src[...] += part[target, rows]
                copies.append(
                    send(
                        src, down.at[step, rows], send_sem.at[piece, 4 + step], recv_sem.at[piece, 4 + step], me.z_peer(1)
                    )
                )
            else:
                copies.append(held[piece][1])
            held[piece] = copies
            pending.extend(copies if step < 3 else copies[:1])
        between(step)

    def before(piece):
        rows = pl.ds(piece * SUB, SUB)
        held[piece][0].wait_recv()
        held[piece][1].wait_recv()
        finish(piece, part[me.r, rows] + up[3, rows] + down[2, rows])

    return before, pending


def scatter_col(me, part, other, summed, inbox, inbox2, totals, sems, compute):
    send_sem, recv_sem = sems
    pending = []
    order = [(me.y + i) % SIDE for i in (1, 2, 3, 0)]
    crossing = []
    for i, y in enumerate(order):
        compute(1 - me.k, y)
        crossing.append(send(part.at[1 - me.k, y], other.at[y], send_sem.at[i], recv_sem.at[i], me.sibling()))
    for y in order:
        compute(me.k, y)
    pending.extend(crossing)
    low, high = pl.ds(0, HALF), pl.ds(HALF, HALF)
    first = []
    for i, y in enumerate(order):
        crossing[i].wait_recv()
        for x in range(SIDE):
            summed[y, x] = (part[me.k, y, x] + other[y, x]).astype(summed.dtype)
        if i < 3:
            n = 4 + i
            first.append(
                send(summed.at[y, :, high], inbox.at[1, i], send_sem.at[n], recv_sem.at[n], me.y_peer(i + 1))
            )
    for i in range(3):
        n = 7 + i
        x = (me.x + i + 1) % SIDE
        first.append(send(summed.at[:, x, low], inbox.at[0, i], send_sem.at[n], recv_sem.at[n], me.x_peer(i + 1)))
    for copy in first:
        copy.wait_recv()
    pending.extend(first)
    second = []
    for i in (1, 2, 3, 0):
        y, x = (me.y + i) % SIDE, (me.x + i) % SIDE
        total = summed[y, me.x, low].astype(F32)
        for j in range(3):
            total += inbox[0, j, y].astype(F32)
        totals[0, y] = total.astype(totals.dtype)
        if i:
            n = 9 + i
            second.append(
                send(totals.at[0, y], inbox2.at[0, i - 1], send_sem.at[n], recv_sem.at[n], me.y_peer(i))
            )
        total = summed[me.y, x, high].astype(F32)
        for j in range(3):
            total += inbox[1, j, x].astype(F32)
        totals[1, x] = total.astype(totals.dtype)
        if i:
            n = 12 + i
            second.append(
                send(totals.at[1, x], inbox2.at[1, i - 1], send_sem.at[n], recv_sem.at[n], me.x_peer(i))
            )
    for copy in second:
        copy.wait_recv()
    pending.extend(second)
    halves = []
    for h, mine in enumerate((me.y, me.x)):
        total = totals[h, mine].astype(F32)
        for j in range(3):
            total += inbox2[h, j].astype(F32)
        halves.append(total)
    return halves, pending


def gather_col(me, full, sems, between=(lambda: None, lambda: None, lambda: None)):
    send_sem, recv_sem = sems
    pending = []
    k, y, x = me.k, me.y, me.x
    low, high = pl.ds(0, HALF), pl.ds(HALF, HALF)
    first = []
    for i in (1, 2, 3):
        block = full.at[k, y, x, low]
        first.append(send(block, block, send_sem.at[i - 1], recv_sem.at[i - 1], me.y_peer(i)))
        block = full.at[k, y, x, high]
        first.append(send(block, block, send_sem.at[i + 2], recv_sem.at[i + 2], me.x_peer(i)))
    between[0]()
    for copy in first:
        copy.wait_recv()
    pending.extend(first)
    second = []
    for i in (1, 2, 3):
        block = full.at[k, :, x, low]
        second.append(send(block, block, send_sem.at[i + 5], recv_sem.at[i + 5], me.x_peer(i)))
        block = full.at[k, y, :, high]
        second.append(send(block, block, send_sem.at[i + 8], recv_sem.at[i + 8], me.y_peer(i)))
    third = []

    def cross(n, block):
        third.append(send(block, block, send_sem.at[n], recv_sem.at[n], me.sibling()))

    cross(12, full.at[k, :, x, low])
    cross(13, full.at[k, y, :, high])
    between[1]()
    for i in (1, 3, 2):
        second[2 * i - 2].wait_recv()
        cross(13 + i, full.at[k, :, (x - i + SIDE) % SIDE, low])
        second[2 * i - 1].wait_recv()
        cross(16 + i, full.at[k, (y - i + SIDE) % SIDE, :, high])
    pending.extend(second)
    between[2]()
    for copy in third:
        copy.wait_recv()
    pending.extend(third)
    return pending


def dot(a, b, contract, precision=None):
    return lax.dot_general(a, b, ((contract[:1], contract[1:]), ((), ())), precision=precision, preferred_element_type=F32)


def forward(operand, matrix, part):
    def compute(core, y):
        for half in range(2):
            start = pl.multiple_of((core * 16 + y * 4 + half * 2) * CHUNK, 256)
            out = dot(operand[...], matrix[pl.ds(start, 256), :], (1, 1))
            part[core, y, 2 * half] = out[:, :CHUNK]
            part[core, y, 2 * half + 1] = out[:, CHUNK:]

    return compute


def flatten(full, flat):
    def body(n, carry):
        core, y, x = n // 16, (n // 4) % 4, n % 4
        flat[:, pl.ds(pl.multiple_of(n * CHUNK, CHUNK), CHUNK)] = full[core, y, x]
        return carry

    lax.fori_loop(0, 32, body, 0)


def backward(flat, matrix, part):
    def body(n, carry):
        start = pl.multiple_of(n * 256, 256)
        out = dot(flat[...], matrix[:, pl.ds(start, 256)], (1, 0))
        part[2 * n] = out[:, :CHUNK]
        part[2 * n + 1] = out[:, CHUNK:]
        return carry

    lax.fori_loop(0, 4, body, 0)


def packed_tiles():
    return [(g, t) for g in range(36) for t in range((g * 8 + 7) // CHUNK + 1)]


def sample_kernel(
    blocks_ref, slot_ref, sketch_ref, basis_ref, projected_ref,
    tiles, matrix, operand, middle, part, other, sum_f, inbox_f, inbox2_f, totals_f,
    sum_h, inbox_h, inbox2_h, totals_h, full, full2, flat, zpart, up, down, up2, down2, gram, packed, gathered, sums, sums_z,
    power, work, right_side,
    ga_s, ga_r, gb_s, gb_r, za_s, za_r, zb_s, zb_r, ca_s, ca_r, cb_s, cb_r, fa_s, fa_r, fb_s, fb_r,
    g1_s, g1_r, g2_s, g2_r, g3_s, g3_r, local,
):
    me = Place()
    pending = []
    load = pltpu.make_async_copy(blocks_ref, tiles.at[pl.ds(0, SLOTS)], local.at[0])
    load.start()
    operand[:, lanes(me.r)] = sketch_ref[...]
    tiles[SLOTS] = jnp.zeros((CHUNK, CHUNK), BF16)
    greet([me.col_peer(i) for i in range(1, 32)] + [me.z_peer(i) for i in range(1, NZ)])

    def build(n, carry):
        start = pl.multiple_of(((n % 2) * 16 + n // 2) * CHUNK, CHUNK)
        for t in range(8):
            matrix[pl.ds(start, CHUNK), t * CHUNK : (t + 1) * CHUNK] = tiles[slot_ref[n * 8 + t]]
        return carry

    def build_all():
        load.wait()
        lax.fori_loop(0, 32, build, 0)

    pending += gather_z(me, operand, (ga_s, ga_r), lambda piece: None, build_all)

    halves, more = scatter_col(
        me, part, other, sum_f, inbox_f, inbox2_f, totals_f, (ca_s, ca_r), forward(operand, matrix, part)
    )
    for copy in more:
        copy.wait_send()
    full[me.k, me.y, me.x, pl.ds(0, HALF)] = halves[0].astype(BF16)
    full[me.k, me.y, me.x, pl.ds(HALF, HALF)] = halves[1].astype(BF16)
    pending += gather_col(me, full, (fa_s, fa_r))
    flatten(full, flat)
    backward(flat, matrix, zpart)

    def finish(piece, total):
        middle[pl.ds(piece * SUB, SUB), lanes(me.r)] = total.astype(BF16)

    before, more = scatter_z(me, zpart, up, down, (za_s, za_r), finish)
    pending += gather_z(me, middle, (gb_s, gb_r), before)
    for copy in more:
        copy.wait_send()

    halves, more = scatter_col(
        me, part, other, sum_h, inbox_h, inbox2_h, totals_h, (cb_s, cb_r), forward(middle, matrix, part)
    )
    pending += more
    power[pl.ds(0, HALF)] = halves[0]
    power[pl.ds(HALF, HALF)] = halves[1]
    full2[me.k, me.y, me.x, pl.ds(0, HALF)] = halves[0].astype(BF16)
    full2[me.k, me.y, me.x, pl.ds(HALF, HALF)] = halves[1].astype(BF16)

    sent = []

    def gram_part():
        gram[...] = jnp.zeros_like(gram)
        gram[:, 0:WIDTH] = dot(power[...], power[...], (1, 1), HIGHEST)
        for n, (g, t) in enumerate(packed_tiles()):
            packed[n] = gram[g * 8 : g * 8 + 8, t * CHUNK : (t + 1) * CHUNK]
        for n in range(len(packed_tiles()), PACKED):
            packed[n] = jnp.zeros((8, CHUNK), F32)
        for i in range(1, 32):
            sent.append(
                send(packed.at[pl.ds(2 * ((me.c + i) % 32), 2)], gathered.at[me.c], g1_s.at[i], g1_r.at[i], me.col_peer(i))
            )

    def gram_col():
        for copy in sent:
            copy.wait_recv()
        gathered[me.c] = packed[pl.ds(2 * me.c, 2)]
        total = gathered[0]
        for i in range(1, 32):
            total += gathered[i]
        sums_z[me.r] = total
        pending.extend(sent)
        sent.clear()
        for i in (4, 3, 5, 2, 6, 1, 7):
            sent.append(send(sums_z.at[me.r], sums_z.at[me.r], g2_s.at[i], g2_r.at[i], me.z_peer(i)))

    def gram_row():
        for copy in sent:
            copy.wait_recv()
        total = sums_z[0]
        for i in range(1, NZ):
            total += sums_z[i]
        sums[me.c] = total
        pending.extend(sent)
        sent.clear()
        for i in range(1, 32):
            sent.append(send(sums.at[me.c], sums.at[me.c], g3_s.at[i], g3_r.at[i], me.col_peer(i)))

    pending += gather_col(me, full2, (fb_s, fb_r), (gram_part, gram_col, gram_row))
    pending.extend(sent)
    flatten(full2, flat)
    backward(flat, matrix, zpart)

    def keep(piece, total):
        right_side[piece * SUB : (piece + 1) * SUB, CHUNK:] = total

    def between(step):
        if step == 0:
            for copy in sent:
                copy.wait_recv()
            unpack_gram(sums, work)
        for panel in (2 * step, 2 * step + 1):
            eliminate(work, panel)

    before, more = scatter_z(me, zpart, up2, down2, (zb_s, zb_r), keep, between)
    pending += more
    eliminate(work, 8)
    right_side[0:WIDTH, 0:CHUNK] = power[...]
    right_side[WIDTH:] = jnp.zeros((384 - WIDTH, 2 * CHUNK), F32)
    for piece in range(NSUB):
        before(piece)
    out = dot(work[0:WIDTH, 384:], right_side[...], (1, 0), HIGHEST)
    basis_ref[...] = out[:, :CHUNK]
    projected_ref[...] = out[:, CHUNK:]
    for copy in pending:
        copy.wait_send()


def over_lanes(block, lane):
    return jnp.broadcast_to(block[:, lane : lane + 1], (8, CHUNK))


def over_rows(block, row):
    return jnp.broadcast_to(block[row : row + 1, :], (8, CHUNK))


def invert_factor(left, off):
    row = lax.broadcasted_iota(jnp.int32, (8, CHUNK), 0)
    lane = lax.broadcasted_iota(jnp.int32, (8, CHUNK), 1)
    L = [left[8 * h : 8 * h + 8] for h in range(4)]
    R = [(lane == row + 8 * h + off).astype(F32) for h in range(4)]
    for g in range(4):
        cols = {h: [over_lanes(L[h], off + 8 * g + b) for b in range(8)] for h in range(g, 4)}
        p = [[over_rows(cols[g][b], a) for b in range(a + 1)] for a in range(8)]
        left_rows = [over_rows(L[g], a) for a in range(8)]
        right_rows = [over_rows(R[g], a) for a in range(8)]
        for b in range(8):
            inv = lax.rsqrt(p[b][b])
            for a in range(b + 1, 8):
                p[a][b] = p[a][b] * inv
            for a in range(b + 1, 8):
                for c in range(b + 1, a + 1):
                    p[a][c] = p[a][c] - p[a][b] * p[c][b]
            left_rows[b] = left_rows[b] * inv
            right_rows[b] = right_rows[b] * inv
            for a in range(b + 1, 8):
                left_rows[a] = left_rows[a] - p[a][b] * left_rows[b]
                right_rows[a] = right_rows[a] - p[a][b] * right_rows[b]
            for h in range(g + 1, 4):
                cols[h][b] = cols[h][b] * inv
                for a in range(b + 1, 8):
                    cols[h][a] = cols[h][a] - p[a][b] * cols[h][b]
        for h in range(g + 1, 4):
            for b in range(8):
                L[h] = L[h] - cols[h][b] * left_rows[b]
                R[h] = R[h] - cols[h][b] * right_rows[b]
        new = right_rows[0]
        for a in range(1, 8):
            new = jnp.where(row == a, right_rows[a], new)
        R[g] = new
    return jnp.concatenate(R, 0)


def unpack_gram(sums, work):
    work[...] = jnp.zeros_like(work)
    for n, (g, t) in enumerate(packed_tiles()):
        work[g * 8 : g * 8 + 8, t * CHUNK : (t + 1) * CHUNK] = sums[n // 2, n % 2] * (1.0 / 32768.0)
    work[0:128, 128:256] = work[128:256, 0:128].T
    work[0:128, 256:384] = work[256:384, 0:128].T
    work[128:256, 256:384] = work[256:384, 128:256].T
    row = lax.broadcasted_iota(jnp.int32, (CHUNK, CHUNK), 0)
    lane = lax.broadcasted_iota(jnp.int32, (CHUNK, CHUNK), 1)
    one = (row == lane).astype(F32)
    for t in range(3):
        work[t * CHUNK : (t + 1) * CHUNK, 384 + t * CHUNK : 384 + (t + 1) * CHUNK] = one


def eliminate(work, panel):
    r0 = panel * 32
    tile, off = r0 // CHUNK, r0 % CHUNK
    block = slice(tile * CHUNK, (tile + 1) * CHUNK)
    span = slice(tile * CHUNK, 384 + (tile + 1) * CHUNK)
    right = invert_factor(work[r0 : r0 + 32, block], off)
    upper = dot(right, work[block, span], (1, 0), HIGHEST)
    if panel < 8:
        lower = dot(work[r0 + 32 : WIDTH, block], right, (1, 1), HIGHEST)
        work[r0 + 32 : WIDTH, span] -= dot(lower, upper, (1, 0), HIGHEST)
    work[r0 : r0 + 32, 384 : 384 + (tile + 1) * CHUNK] = upper[:, 384 - tile * CHUNK :]


def sem(*shape):
    return [DMA(shape), DMA(shape)]


def local(blocks, positions, counts, sketch):
    places = positions[0, 0]
    used = lax.iota(jnp.int32, SLOTS) < counts[0, 0]
    where = jnp.where(used, places, -1)
    hit = where[None, :] == lax.iota(jnp.int32, 256)[:, None]
    slots = jnp.min(jnp.where(hit, lax.iota(jnp.int32, SLOTS)[None, :], SLOTS), axis=1)

    vmem = pl.BlockSpec(memory_space=pltpu.VMEM)
    hbm = pl.BlockSpec(memory_space=pl.ANY)
    smem = pl.BlockSpec(memory_space=pltpu.SMEM)
    V = pltpu.VMEM
    basis, projected = pl.pallas_call(
        sample_kernel,
        out_shape=[jax.ShapeDtypeStruct((WIDTH, CHUNK), F32)] * 2,
        in_specs=[hbm, smem, vmem],
        out_specs=[vmem, vmem],
        scratch_shapes=[
            V((SLOTS + 1, CHUNK, CHUNK), BF16),
            V((4096, 1024), BF16),
            V((WIDTH, 1024), BF16),
            V((WIDTH, 1024), BF16),
            V((2, SIDE, SIDE, WIDTH, CHUNK), F32),
            V((SIDE, SIDE, WIDTH, CHUNK), F32),
            V((SIDE, SIDE, WIDTH, CHUNK), F32),
            V((2, 3, SIDE, HALF, CHUNK), F32),
            V((2, 3, HALF, CHUNK), F32),
            V((2, SIDE, HALF, CHUNK), F32),
            V((SIDE, SIDE, WIDTH, CHUNK), BF16),
            V((2, 3, SIDE, HALF, CHUNK), BF16),
            V((2, 3, HALF, CHUNK), BF16),
            V((2, SIDE, HALF, CHUNK), BF16),
            V((2, SIDE, SIDE, WIDTH, CHUNK), BF16),
            V((2, SIDE, SIDE, WIDTH, CHUNK), BF16),
            V((WIDTH, 4096), BF16),
            V((NZ, WIDTH, CHUNK), F32),
            V((4, WIDTH, CHUNK), F32),
            V((3, WIDTH, CHUNK), F32),
            V((4, WIDTH, CHUNK), F32),
            V((3, WIDTH, CHUNK), F32),
            V((WIDTH, 384), F32),
            V((PACKED, 8, CHUNK), F32),
            V((32, 2, 8, CHUNK), F32),
            V((32, 2, 8, CHUNK), F32),
            V((NZ, 2, 8, CHUNK), F32),
            V((WIDTH, CHUNK), F32),
            V((384, 768), F32),
            V((384, 2 * CHUNK), F32),
            *sem(NSUB, 7),
            *sem(NSUB, 7),
            *sem(NSUB, 7),
            *sem(NSUB, 7),
            *sem(16),
            *sem(16),
            *sem(20),
            *sem(20),
            *sem(32),
            *sem(8),
            *sem(32),
            DMA((1,)),
        ],
        compiler_params=pltpu.CompilerParams(
            collective_id=1, has_side_effects=True, vmem_limit_bytes=56 << 20
        ),
    )(blocks[0, 0], slots, sketch.T)

    return (basis.T, projected.T)


def solution(mesh):
    return jax.shard_map(
        local,
        mesh=mesh,
        in_specs=(
            P("row", "col", None, None, None),
            P("row", "col", None),
            P("row", "col"),
            P(("col", "row"), None),
        ),
        out_specs=(P(("row", "col"), None), P(("col", "row"), None)),
        check_vma=False,
    )
```

```python
import functools

import jax
import jax.numpy as jnp
from jax import lax
from jax.experimental import pallas as pl
from jax.experimental.pallas import tpu as pltpu
from jax.sharding import PartitionSpec as P

MESH = pl.DeviceIdType.MESH
F32 = jnp.float32
BF16 = jnp.bfloat16
DMA = pltpu.SemaphoreType.DMA
HIGHEST = lax.Precision.HIGHEST

NZ = 8
SIDE = 4
CHUNK = 128
WIDTH = 288
HALF = 144
SUB = 96
NSUB = WIDTH // SUB
SLOTS = 96
PACKED = 64


class Place:
    def __init__(self):
        self.r = lax.axis_index("row")
        self.c = lax.axis_index("col")
        self.y = self.c // 8
        self.x = (self.c // 2) % SIDE
        self.k = self.c % 2

    def x_peer(self, i):
        return (self.r, (self.y * SIDE + (self.x + i) % SIDE) * 2 + self.k)

    def y_peer(self, i):
        return (self.r, (((self.y + i) % SIDE) * SIDE + self.x) * 2 + self.k)

    def sibling(self):
        return (self.r, self.c + 1 - 2 * self.k)

    def z_peer(self, i):
        return ((self.r + i) % NZ, self.c)

    def col_peer(self, i):
        return (self.r, (self.c + i) % 32)


def greet(peers):
    barrier = pltpu.get_barrier_semaphore()
    for peer in peers:
        pl.semaphore_signal(barrier, inc=1, device_id=peer, device_id_type=MESH)
    pl.semaphore_wait(barrier, len(peers))


def send(src, dst, send_sem, recv_sem, peer):
    copy = pltpu.make_async_remote_copy(
        src_ref=src,
        dst_ref=dst,
        send_sem=send_sem,
        recv_sem=recv_sem,
        device_id=peer,
        device_id_type=MESH,
    )
    copy.start()
    return copy


def lanes(chunk):
    return pl.ds(pl.multiple_of(chunk * CHUNK, CHUNK), CHUNK)


def gather_z_piece(me, full, sems, piece, pending):
    rows = pl.ds(piece * SUB, SUB)
    send_sem, recv_sem = sems

    def go(step, way):
        owner = (me.r - way * step + NZ) % NZ
        block = full.at[rows, lanes(owner)]
        n = (0 if way == 1 else 4) + step
        copy = send(block, block, send_sem.at[piece, n], recv_sem.at[piece, n], me.z_peer(way % NZ))
        pending.append(copy)
        return copy

    return go


def gather_z(me, full, sems, before, meanwhile=None):
    pending = []
    goes = [gather_z_piece(me, full, sems, piece, pending) for piece in range(NSUB)]
    held = {}
    for step in range(4):
        for piece in range(NSUB):
            if step > 0:
                for copy in held[piece]:
                    copy.wait_recv()
            else:
                before(piece)
            copies = [goes[piece](step, 1)]
            if step < 3:
                copies.append(goes[piece](step, -1))
            held[piece] = copies
        if step == 0 and meanwhile is not None:
            meanwhile()
    for piece in range(NSUB):
        for copy in held[piece]:
            copy.wait_recv()
    return pending


def scatter_z(me, part, up, down, sems, finish, between=lambda step: None):
    send_sem, recv_sem = sems
    pending = []
    held = {}
    for step in range(4):
        for piece in range(NSUB):
            rows = pl.ds(piece * SUB, SUB)
            copies = []
            target = (me.r + 4 + step) % NZ
            if step == 0:
                src = part.at[target, rows]
            else:
                held[piece][0].wait_recv()
                src = up.at[step - 1, rows]
                src[...] += part[target, rows]
            copies.append(
                send(src, up.at[step, rows], send_sem.at[piece, step], recv_sem.at[piece, step], me.z_peer(NZ - 1))
            )
            if step < 3:
                target = (me.r + 3 - step) % NZ
                if step == 0:
                    src = part.at[target, rows]
                else:
                    held[piece][1].wait_recv()
                    src = down.at[step - 1, rows]
                    src[...] += part[target, rows]
                copies.append(
                    send(
                        src, down.at[step, rows], send_sem.at[piece, 4 + step], recv_sem.at[piece, 4 + step], me.z_peer(1)
                    )
                )
            else:
                copies.append(held[piece][1])
            held[piece] = copies
            pending.extend(copies if step < 3 else copies[:1])
        between(step)

    def before(piece):
        rows = pl.ds(piece * SUB, SUB)
        held[piece][0].wait_recv()
        held[piece][1].wait_recv()
        finish(piece, part[me.r, rows] + up[3, rows] + down[2, rows])

    return before, pending


def scatter_col(me, part, other, summed, inbox, inbox2, totals, sems, compute):
    send_sem, recv_sem = sems
    pending = []
    order = [(me.y + i) % SIDE for i in (1, 2, 3, 0)]
    crossing = []
    for i, y in enumerate(order):
        compute(1 - me.k, y)
        crossing.append(send(part.at[1 - me.k, y], other.at[y], send_sem.at[i], recv_sem.at[i], me.sibling()))
    for y in order:
        compute(me.k, y)
    pending.extend(crossing)
    low, high = pl.ds(0, HALF), pl.ds(HALF, HALF)
    first, along_x = [], []
    for i, y in enumerate(order):
        crossing[i].wait_recv()
        for x in range(SIDE):
            summed[y, x] = (part[me.k, y, x] + other[y, x]).astype(summed.dtype)
        group = []
        for j in (2, 1, 3):
            n = 7 + 3 * i + j
            x = (me.x + j) % SIDE
            group.append(
                send(summed.at[y, x, low], inbox.at[0, j - 1, i], send_sem.at[n], recv_sem.at[n], me.x_peer(j))
            )
        along_x.append(group)
        if i < 3:
            n = 4 + i
            first.append(
                send(summed.at[y, :, high], inbox.at[1, i], send_sem.at[n], recv_sem.at[n], me.y_peer(i + 1))
            )
    second = []
    for i, y in enumerate(order):
        for copy in along_x[i]:
            copy.wait_recv()
        pending.extend(along_x[i])
        total = summed[y, me.x, low].astype(F32)
        for j in range(3):
            total += inbox[0, j, i].astype(F32)
        totals[0, y] = total.astype(totals.dtype)
        if i < 3:
            n = 20 + i
            second.append(send(totals.at[0, y], inbox2.at[0, i], send_sem.at[n], recv_sem.at[n], me.y_peer(i + 1)))
    for copy in first:
        copy.wait_recv()
    pending.extend(first)
    for i in (2, 1, 3, 0):
        x = (me.x + i) % SIDE
        total = summed[me.y, x, high].astype(F32)
        for j in range(3):
            total += inbox[1, j, x].astype(F32)
        totals[1, x] = total.astype(totals.dtype)
        if i:
            n = 22 + i
            second.append(
                send(totals.at[1, x], inbox2.at[1, i - 1], send_sem.at[n], recv_sem.at[n], me.x_peer(i))
            )
    for copy in second:
        copy.wait_recv()
    pending.extend(second)
    halves = []
    for h, mine in enumerate((me.y, me.x)):
        total = totals[h, mine].astype(F32)
        for j in range(3):
            total += inbox2[h, j].astype(F32)
        halves.append(total)
    return halves, pending


def gather_col(me, full, sems, between=(lambda: None, lambda: None, lambda: None)):
    send_sem, recv_sem = sems
    pending = []
    k, y, x = me.k, me.y, me.x
    low, high = pl.ds(0, HALF), pl.ds(HALF, HALF)
    own_low, own_high = full.at[k, y, x, low], full.at[k, y, x, high]
    count = [0]

    def start(block, peer):
        n = count[0]
        count[0] += 1
        copy = send(block, block, send_sem.at[n], recv_sem.at[n], peer)
        pending.append(copy)
        return copy

    first = [(start(own_low, me.y_peer(i)), start(own_high, me.x_peer(i))) for i in (1, 2, 3)]
    second = {i: [start(own_low, me.x_peer(i)), start(own_high, me.y_peer(i))] for i in (1, 2, 3)}
    third = [start(full.at[k, y, x], me.sibling())]
    between[0]()
    for i in (1, 2, 3):
        first[i - 1][0].wait_recv()
        block = full.at[k, (y - i + SIDE) % SIDE, x, low]
        for j in (2, 1, 3):
            second[j].append(start(block, me.x_peer(j)))
        third.append(start(block, me.sibling()))
        first[i - 1][1].wait_recv()
        block = full.at[k, y, (x - i + SIDE) % SIDE, high]
        for j in (2, 1, 3):
            second[j].append(start(block, me.y_peer(j)))
        third.append(start(block, me.sibling()))
    between[1]()
    for i in (1, 3, 2):
        for copy in second[i]:
            copy.wait_recv()
        third.append(start(full.at[k, :, (x - i + SIDE) % SIDE, low], me.sibling()))
        third.append(start(full.at[k, (y - i + SIDE) % SIDE, :, high], me.sibling()))
    between[2]()
    for copy in third:
        copy.wait_recv()
    return pending


def dot(a, b, contract, precision=None):
    return lax.dot_general(a, b, ((contract[:1], contract[1:]), ((), ())), precision=precision, preferred_element_type=F32)


def forward(operand, matrix, part):
    def compute(core, y):
        for half in range(2):
            start = pl.multiple_of((core * 16 + y * 4 + half * 2) * CHUNK, 256)
            out = dot(operand[...], matrix[pl.ds(start, 256), :], (1, 1))
            part[core, y, 2 * half] = out[:, :CHUNK]
            part[core, y, 2 * half + 1] = out[:, CHUNK:]

    return compute


def backward(full, flat, matrix, part, core, first):
    start = pl.multiple_of(core * 2048, 2048)

    def flatten(n, carry):
        flat[:, pl.ds(pl.multiple_of(n * CHUNK, CHUNK), CHUNK)] = full[core, n // SIDE, n % SIDE]
        return carry

    lax.fori_loop(0, 16, flatten, 0)

    def body(n, carry):
        out = dot(flat[...], matrix[pl.ds(start, 2048), pl.ds(pl.multiple_of(n * 256, 256), 256)], (1, 0))
        for half in range(2):
            share = out[:, half * CHUNK : (half + 1) * CHUNK]
            part[2 * n + half] = share if first else part[2 * n + half] + share
        return carry

    lax.fori_loop(0, 4, body, 0)


def packed_tiles():
    return [(g, t) for g in range(36) for t in range((g * 8 + 7) // CHUNK + 1)]


def sample_kernel(
    blocks_ref, slot_ref, sketch_ref, basis_ref, projected_ref,
    tiles, matrix, operand, middle, part, other, sum_f, inbox_f, inbox2_f, totals_f,
    sum_h, inbox_h, inbox2_h, totals_h, full, full2, flat, zpart, up, down, up2, down2, gram, packed, gathered, sums, sums_z,
    power, work, right_side,
    ga_s, ga_r, gb_s, gb_r, za_s, za_r, zb_s, zb_r, ca_s, ca_r, cb_s, cb_r, fa_s, fa_r, fb_s, fb_r,
    g1_s, g1_r, g2_s, g2_r, g3_s, g3_r, local,
):
    me = Place()
    pending = []
    load = pltpu.make_async_copy(blocks_ref, tiles.at[pl.ds(0, SLOTS)], local.at[0])
    load.start()
    operand[:, lanes(me.r)] = sketch_ref[...]
    tiles[SLOTS] = jnp.zeros((CHUNK, CHUNK), BF16)
    greet([me.col_peer(i) for i in range(1, 32)] + [me.z_peer(i) for i in range(1, NZ)])

    def build(n, carry):
        start = pl.multiple_of(((n % 2) * 16 + n // 2) * CHUNK, CHUNK)
        for t in range(8):
            matrix[pl.ds(start, CHUNK), t * CHUNK : (t + 1) * CHUNK] = tiles[slot_ref[n * 8 + t]]
        return carry

    def build_all():
        load.wait()
        lax.fori_loop(0, 32, build, 0)

    pending += gather_z(me, operand, (ga_s, ga_r), lambda piece: None, build_all)

    halves, more = scatter_col(
        me, part, other, sum_f, inbox_f, inbox2_f, totals_f, (ca_s, ca_r), forward(operand, matrix, part)
    )
    for copy in more:
        copy.wait_send()
    full[me.k, me.y, me.x, pl.ds(0, HALF)] = halves[0].astype(BF16)
    full[me.k, me.y, me.x, pl.ds(HALF, HALF)] = halves[1].astype(BF16)
    hooks = (lambda: None, lambda: None, lambda: backward(full, flat, matrix, zpart, me.k, True))
    pending += gather_col(me, full, (fa_s, fa_r), hooks)
    backward(full, flat, matrix, zpart, 1 - me.k, False)

    def finish(piece, total):
        middle[pl.ds(piece * SUB, SUB), lanes(me.r)] = total.astype(BF16)

    before, more = scatter_z(me, zpart, up, down, (za_s, za_r), finish)
    pending += gather_z(me, middle, (gb_s, gb_r), before)
    for copy in more:
        copy.wait_send()

    halves, more = scatter_col(
        me, part, other, sum_h, inbox_h, inbox2_h, totals_h, (cb_s, cb_r), forward(middle, matrix, part)
    )
    pending += more
    power[pl.ds(0, HALF)] = halves[0]
    power[pl.ds(HALF, HALF)] = halves[1]
    full2[me.k, me.y, me.x, pl.ds(0, HALF)] = halves[0].astype(BF16)
    full2[me.k, me.y, me.x, pl.ds(HALF, HALF)] = halves[1].astype(BF16)

    sent = []

    def gram_part():
        gram[...] = jnp.zeros_like(gram)
        gram[:, 0:WIDTH] = dot(power[...], power[...], (1, 1), HIGHEST)
        for n, (g, t) in enumerate(packed_tiles()):
            packed[n] = gram[g * 8 : g * 8 + 8, t * CHUNK : (t + 1) * CHUNK]
        for n in range(len(packed_tiles()), PACKED):
            packed[n] = jnp.zeros((8, CHUNK), F32)
        for i in range(1, 32):
            sent.append(
                send(packed.at[pl.ds(2 * ((me.c + i) % 32), 2)], gathered.at[me.c], g1_s.at[i], g1_r.at[i], me.col_peer(i))
            )

    def gram_col():
        for copy in sent:
            copy.wait_recv()
        gathered[me.c] = packed[pl.ds(2 * me.c, 2)]
        total = gathered[0]
        for i in range(1, 32):
            total += gathered[i]
        sums_z[me.r] = total
        pending.extend(sent)
        sent.clear()
        for i in (4, 3, 5, 2, 6, 1, 7):
            sent.append(send(sums_z.at[me.r], sums_z.at[me.r], g2_s.at[i], g2_r.at[i], me.z_peer(i)))

    def gram_row():
        for copy in sent:
            copy.wait_recv()
        total = sums_z[0]
        for i in range(1, NZ):
            total += sums_z[i]
        sums[me.c] = total
        pending.extend(sent)
        sent.clear()
        for i in range(1, 32):
            sent.append(send(sums.at[me.c], sums.at[me.c], g3_s.at[i], g3_r.at[i], me.col_peer(i)))

    def gram_row_and_pass():
        gram_row()
        backward(full2, flat, matrix, zpart, me.k, True)

    pending += gather_col(me, full2, (fb_s, fb_r), (gram_part, gram_col, gram_row_and_pass))
    pending.extend(sent)
    backward(full2, flat, matrix, zpart, 1 - me.k, False)

    def keep(piece, total):
        right_side[piece * SUB : (piece + 1) * SUB, CHUNK:] = total

    def between(step):
        if step == 0:
            for copy in sent:
                copy.wait_recv()
            unpack_gram(sums, work)
        for panel in (2 * step, 2 * step + 1):
            eliminate(work, panel)

    before, more = scatter_z(me, zpart, up2, down2, (zb_s, zb_r), keep, between)
    pending += more
    eliminate(work, 8)
    right_side[0:WIDTH, 0:CHUNK] = power[...]
    right_side[WIDTH:] = jnp.zeros((384 - WIDTH, 2 * CHUNK), F32)
    for piece in range(NSUB):
        before(piece)
    out = dot(work[0:WIDTH, 384:], right_side[...], (1, 0), HIGHEST)
    basis_ref[...] = out[:, :CHUNK]
    projected_ref[...] = out[:, CHUNK:]
    for copy in pending:
        copy.wait_send()


def over_lanes(block, lane):
    return jnp.broadcast_to(block[:, lane : lane + 1], (8, CHUNK))


def over_rows(block, row):
    return jnp.broadcast_to(block[row : row + 1, :], (8, CHUNK))


def invert_factor(left, off):
    row = lax.broadcasted_iota(jnp.int32, (8, CHUNK), 0)
    lane = lax.broadcasted_iota(jnp.int32, (8, CHUNK), 1)
    L = [left[8 * h : 8 * h + 8] for h in range(4)]
    R = [(lane == row + 8 * h + off).astype(F32) for h in range(4)]
    for g in range(4):
        cols = {h: [over_lanes(L[h], off + 8 * g + b) for b in range(8)] for h in range(g, 4)}
        p = [[over_rows(cols[g][b], a) for b in range(a + 1)] for a in range(8)]
        left_rows = [over_rows(L[g], a) for a in range(8)]
        right_rows = [over_rows(R[g], a) for a in range(8)]
        for b in range(8):
            inv = lax.rsqrt(p[b][b])
            for a in range(b + 1, 8):
                p[a][b] = p[a][b] * inv
            for a in range(b + 1, 8):
                for c in range(b + 1, a + 1):
                    p[a][c] = p[a][c] - p[a][b] * p[c][b]
            left_rows[b] = left_rows[b] * inv
            right_rows[b] = right_rows[b] * inv
            for a in range(b + 1, 8):
                left_rows[a] = left_rows[a] - p[a][b] * left_rows[b]
                right_rows[a] = right_rows[a] - p[a][b] * right_rows[b]
            for h in range(g + 1, 4):
                cols[h][b] = cols[h][b] * inv
                for a in range(b + 1, 8):
                    cols[h][a] = cols[h][a] - p[a][b] * cols[h][b]
        for h in range(g + 1, 4):
            for b in range(8):
                L[h] = L[h] - cols[h][b] * left_rows[b]
                R[h] = R[h] - cols[h][b] * right_rows[b]
        new = right_rows[0]
        for a in range(1, 8):
            new = jnp.where(row == a, right_rows[a], new)
        R[g] = new
    return jnp.concatenate(R, 0)


def unpack_gram(sums, work):
    work[...] = jnp.zeros_like(work)
    for n, (g, t) in enumerate(packed_tiles()):
        work[g * 8 : g * 8 + 8, t * CHUNK : (t + 1) * CHUNK] = sums[n // 2, n % 2] * (1.0 / 32768.0)
    work[0:128, 128:256] = work[128:256, 0:128].T
    work[0:128, 256:384] = work[256:384, 0:128].T
    work[128:256, 256:384] = work[256:384, 128:256].T
    row = lax.broadcasted_iota(jnp.int32, (CHUNK, CHUNK), 0)
    lane = lax.broadcasted_iota(jnp.int32, (CHUNK, CHUNK), 1)
    one = (row == lane).astype(F32)
    for t in range(3):
        work[t * CHUNK : (t + 1) * CHUNK, 384 + t * CHUNK : 384 + (t + 1) * CHUNK] = one


def eliminate(work, panel):
    r0 = panel * 32
    tile, off = r0 // CHUNK, r0 % CHUNK
    block = slice(tile * CHUNK, (tile + 1) * CHUNK)
    span = slice(tile * CHUNK, 384 + (tile + 1) * CHUNK)
    right = invert_factor(work[r0 : r0 + 32, block], off)
    upper = dot(right, work[block, span], (1, 0), HIGHEST)
    if panel < 8:
        lower = dot(work[r0 + 32 : WIDTH, block], right, (1, 1), HIGHEST)
        work[r0 + 32 : WIDTH, span] -= dot(lower, upper, (1, 0), HIGHEST)
    work[r0 : r0 + 32, 384 : 384 + (tile + 1) * CHUNK] = upper[:, 384 - tile * CHUNK :]


def sem(*shape):
    return [DMA(shape), DMA(shape)]


def local(blocks, positions, counts, sketch):
    places = positions[0, 0]
    used = lax.iota(jnp.int32, SLOTS) < counts[0, 0]
    where = jnp.where(used, places, -1)
    hit = where[None, :] == lax.iota(jnp.int32, 256)[:, None]
    slots = jnp.min(jnp.where(hit, lax.iota(jnp.int32, SLOTS)[None, :], SLOTS), axis=1)

    vmem = pl.BlockSpec(memory_space=pltpu.VMEM)
    hbm = pl.BlockSpec(memory_space=pl.ANY)
    smem = pl.BlockSpec(memory_space=pltpu.SMEM)
    V = pltpu.VMEM
    basis, projected = pl.pallas_call(
        sample_kernel,
        out_shape=[jax.ShapeDtypeStruct((WIDTH, CHUNK), F32)] * 2,
        in_specs=[hbm, smem, vmem],
        out_specs=[vmem, vmem],
        scratch_shapes=[
            V((SLOTS + 1, CHUNK, CHUNK), BF16),
            V((4096, 1024), BF16),
            V((WIDTH, 1024), BF16),
            V((WIDTH, 1024), BF16),
            V((2, SIDE, SIDE, WIDTH, CHUNK), F32),
            V((SIDE, SIDE, WIDTH, CHUNK), F32),
            V((SIDE, SIDE, WIDTH, CHUNK), F32),
            V((2, 3, SIDE, HALF, CHUNK), F32),
            V((2, 3, HALF, CHUNK), F32),
            V((2, SIDE, HALF, CHUNK), F32),
            V((SIDE, SIDE, WIDTH, CHUNK), BF16),
            V((2, 3, SIDE, HALF, CHUNK), BF16),
            V((2, 3, HALF, CHUNK), BF16),
            V((2, SIDE, HALF, CHUNK), BF16),
            V((2, SIDE, SIDE, WIDTH, CHUNK), BF16),
            V((2, SIDE, SIDE, WIDTH, CHUNK), BF16),
            V((WIDTH, 2048), BF16),
            V((NZ, WIDTH, CHUNK), F32),
            V((4, WIDTH, CHUNK), F32),
            V((3, WIDTH, CHUNK), F32),
            V((4, WIDTH, CHUNK), F32),
            V((3, WIDTH, CHUNK), F32),
            V((WIDTH, 384), F32),
            V((PACKED, 8, CHUNK), F32),
            V((32, 2, 8, CHUNK), F32),
            V((32, 2, 8, CHUNK), F32),
            V((NZ, 2, 8, CHUNK), F32),
            V((WIDTH, CHUNK), F32),
            V((384, 768), F32),
            V((384, 2 * CHUNK), F32),
            *sem(NSUB, 7),
            *sem(NSUB, 7),
            *sem(NSUB, 7),
            *sem(NSUB, 7),
            *sem(26),
            *sem(26),
            *sem(43),
            *sem(43),
            *sem(32),
            *sem(8),
            *sem(32),
            DMA((1,)),
        ],
        compiler_params=pltpu.CompilerParams(
            collective_id=1, has_side_effects=True, vmem_limit_bytes=56 << 20
        ),
    )(blocks[0, 0], slots, sketch.T)

    return (basis.T, projected.T)


def solution(mesh):
    return jax.shard_map(
        local,
        mesh=mesh,
        in_specs=(
            P("row", "col", None, None, None),
            P("row", "col", None),
            P("row", "col"),
            P(("col", "row"), None),
        ),
        out_specs=(P(("row", "col"), None), P(("col", "row"), None)),
        check_vma=False,
    )
```

```python
import functools

import jax
import jax.numpy as jnp
from jax import lax
from jax.experimental import pallas as pl
from jax.experimental.pallas import tpu as pltpu
from jax.sharding import PartitionSpec as P

MESH = pl.DeviceIdType.MESH
F32 = jnp.float32
BF16 = jnp.bfloat16
DMA = pltpu.SemaphoreType.DMA
HIGHEST = lax.Precision.HIGHEST

NZ = 8
SIDE = 4
CHUNK = 128
WIDTH = 288
HALF = 144
SUB = 96
NSUB = WIDTH // SUB
SLOTS = 96
PACKED = 64


class Place:
    def __init__(self):
        self.r = lax.axis_index("row")
        self.c = lax.axis_index("col")
        self.y = self.c // 8
        self.x = (self.c // 2) % SIDE
        self.k = self.c % 2

    def x_peer(self, i):
        return (self.r, (self.y * SIDE + (self.x + i) % SIDE) * 2 + self.k)

    def y_peer(self, i):
        return (self.r, (((self.y + i) % SIDE) * SIDE + self.x) * 2 + self.k)

    def sibling(self):
        return (self.r, self.c + 1 - 2 * self.k)

    def z_peer(self, i):
        return ((self.r + i) % NZ, self.c)

    def col_peer(self, i):
        return (self.r, (self.c + i) % 32)


def greet(peers):
    barrier = pltpu.get_barrier_semaphore()
    for peer in peers:
        pl.semaphore_signal(barrier, inc=1, device_id=peer, device_id_type=MESH)
    pl.semaphore_wait(barrier, len(peers))


def send(src, dst, send_sem, recv_sem, peer):
    copy = pltpu.make_async_remote_copy(
        src_ref=src,
        dst_ref=dst,
        send_sem=send_sem,
        recv_sem=recv_sem,
        device_id=peer,
        device_id_type=MESH,
    )
    copy.start()
    return copy


def lanes(chunk):
    return pl.ds(pl.multiple_of(chunk * CHUNK, CHUNK), CHUNK)


def gather_z_piece(me, full, sems, piece, pending):
    rows = pl.ds(piece * SUB, SUB)
    send_sem, recv_sem = sems

    def go(step, way):
        owner = (me.r - way * step + NZ) % NZ
        block = full.at[rows, lanes(owner)]
        n = (0 if way == 1 else 4) + step
        copy = send(block, block, send_sem.at[piece, n], recv_sem.at[piece, n], me.z_peer(way % NZ))
        pending.append(copy)
        return copy

    return go


def gather_z(me, full, sems, before, meanwhile=None):
    pending = []
    goes = [gather_z_piece(me, full, sems, piece, pending) for piece in range(NSUB)]
    held = {}
    for step in range(4):
        for piece in range(NSUB):
            if step > 0:
                for copy in held[piece]:
                    copy.wait_recv()
            else:
                before(piece)
            copies = [goes[piece](step, 1)]
            if step < 3:
                copies.append(goes[piece](step, -1))
            held[piece] = copies
        if meanwhile is not None:
            meanwhile(step)
    for piece in range(NSUB):
        for copy in held[piece]:
            copy.wait_recv()
    return pending


def scatter_z(me, part, up, down, sems, finish, between=lambda step: None):
    send_sem, recv_sem = sems
    pending = []
    held = {}
    for step in range(4):
        for piece in range(NSUB):
            rows = pl.ds(piece * SUB, SUB)
            copies = []
            target = (me.r + 4 + step) % NZ
            if step == 0:
                src = part.at[target, rows]
            else:
                held[piece][0].wait_recv()
                src = up.at[step - 1, rows]
                src[...] += part[target, rows]
            copies.append(
                send(src, up.at[step, rows], send_sem.at[piece, step], recv_sem.at[piece, step], me.z_peer(NZ - 1))
            )
            if step < 3:
                target = (me.r + 3 - step) % NZ
                if step == 0:
                    src = part.at[target, rows]
                else:
                    held[piece][1].wait_recv()
                    src = down.at[step - 1, rows]
                    src[...] += part[target, rows]
                copies.append(
                    send(
                        src, down.at[step, rows], send_sem.at[piece, 4 + step], recv_sem.at[piece, 4 + step], me.z_peer(1)
                    )
                )
            else:
                copies.append(held[piece][1])
            held[piece] = copies
            pending.extend(copies if step < 3 else copies[:1])
        between(step)

    def before(piece):
        rows = pl.ds(piece * SUB, SUB)
        held[piece][0].wait_recv()
        held[piece][1].wait_recv()
        finish(piece, part[me.r, rows] + up[3, rows] + down[2, rows])

    return before, pending


def scatter_col(me, part, other, summed, inbox, inbox2, totals, sems, compute):
    send_sem, recv_sem = sems
    pending = []
    order = [(me.y + i) % SIDE for i in (1, 2, 3, 0)]
    crossing = []
    for i, y in enumerate(order):
        compute(1 - me.k, y)
        crossing.append(send(part.at[1 - me.k, y], other.at[y], send_sem.at[i], recv_sem.at[i], me.sibling()))
    for y in order:
        compute(me.k, y)
    pending.extend(crossing)
    low, high = pl.ds(0, HALF), pl.ds(HALF, HALF)
    first, along_x = [], []
    for i, y in enumerate(order):
        crossing[i].wait_recv()
        for x in range(SIDE):
            summed[y, x] = (part[me.k, y, x] + other[y, x]).astype(summed.dtype)
        group = []
        for j in (2, 1, 3):
            n = 7 + 3 * i + j
            x = (me.x + j) % SIDE
            group.append(
                send(summed.at[y, x, low], inbox.at[0, j - 1, i], send_sem.at[n], recv_sem.at[n], me.x_peer(j))
            )
        along_x.append(group)
        if i < 3:
            n = 4 + i
            first.append(
                send(summed.at[y, :, high], inbox.at[1, i], send_sem.at[n], recv_sem.at[n], me.y_peer(i + 1))
            )
    second = []
    for i, y in enumerate(order):
        for copy in along_x[i]:
            copy.wait_recv()
        pending.extend(along_x[i])
        total = summed[y, me.x, low].astype(F32)
        for j in range(3):
            total += inbox[0, j, i].astype(F32)
        totals[0, y] = total.astype(totals.dtype)
        if i < 3:
            n = 20 + i
            second.append(send(totals.at[0, y], inbox2.at[0, i], send_sem.at[n], recv_sem.at[n], me.y_peer(i + 1)))
    for copy in first:
        copy.wait_recv()
    pending.extend(first)
    for i in (2, 1, 3, 0):
        x = (me.x + i) % SIDE
        total = summed[me.y, x, high].astype(F32)
        for j in range(3):
            total += inbox[1, j, x].astype(F32)
        totals[1, x] = total.astype(totals.dtype)
        if i:
            n = 22 + i
            second.append(
                send(totals.at[1, x], inbox2.at[1, i - 1], send_sem.at[n], recv_sem.at[n], me.x_peer(i))
            )
    for copy in second:
        copy.wait_recv()
    pending.extend(second)
    halves = []
    for h, mine in enumerate((me.y, me.x)):
        total = totals[h, mine].astype(F32)
        for j in range(3):
            total += inbox2[h, j].astype(F32)
        halves.append(total)
    return halves, pending


def gather_col(me, full, sems, between=(lambda: None, lambda: None, lambda: None)):
    send_sem, recv_sem = sems
    pending = []
    k, y, x = me.k, me.y, me.x
    low, high = pl.ds(0, HALF), pl.ds(HALF, HALF)
    own_low, own_high = full.at[k, y, x, low], full.at[k, y, x, high]
    count = [0]

    def start(block, peer):
        n = count[0]
        count[0] += 1
        copy = send(block, block, send_sem.at[n], recv_sem.at[n], peer)
        pending.append(copy)
        return copy

    first = [(start(own_low, me.y_peer(i)), start(own_high, me.x_peer(i))) for i in (1, 2, 3)]
    second = {i: [start(own_low, me.x_peer(i)), start(own_high, me.y_peer(i))] for i in (1, 2, 3)}
    third = [start(full.at[k, y, x], me.sibling())]
    between[0]()
    for i in (1, 2, 3):
        first[i - 1][0].wait_recv()
        block = full.at[k, (y - i + SIDE) % SIDE, x, low]
        for j in (2, 1, 3):
            second[j].append(start(block, me.x_peer(j)))
        third.append(start(block, me.sibling()))
        first[i - 1][1].wait_recv()
        block = full.at[k, y, (x - i + SIDE) % SIDE, high]
        for j in (2, 1, 3):
            second[j].append(start(block, me.y_peer(j)))
        third.append(start(block, me.sibling()))
    between[1]()
    for i in (1, 3, 2):
        for copy in second[i]:
            copy.wait_recv()
        third.append(start(full.at[k, :, (x - i + SIDE) % SIDE, low], me.sibling()))
        third.append(start(full.at[k, (y - i + SIDE) % SIDE, :, high], me.sibling()))
    between[2]()
    for copy in third:
        copy.wait_recv()
    return pending


def dot(a, b, contract, precision=None):
    return lax.dot_general(a, b, ((contract[:1], contract[1:]), ((), ())), precision=precision, preferred_element_type=F32)


def forward(operand, matrix, part):
    def compute(core, y):
        for half in range(2):
            start = pl.multiple_of((core * 16 + y * 4 + half * 2) * CHUNK, 256)
            out = dot(operand[...], matrix[pl.ds(start, 256), :], (1, 1))
            part[core, y, 2 * half] = out[:, :CHUNK]
            part[core, y, 2 * half + 1] = out[:, CHUNK:]

    return compute


def flatten(full, flat, core):
    def body(n, carry):
        flat[:, pl.ds(pl.multiple_of(n * CHUNK, CHUNK), CHUNK)] = full[core, n // SIDE, n % SIDE]
        return carry

    lax.fori_loop(0, 16, body, 0)


def backward(me, flat, matrix, part, core, first, steps):
    start = pl.multiple_of(core * 2048, 2048)

    def body(step, carry):
        n = (me.r // 2 + 6 - step) % 4
        out = dot(flat[...], matrix[pl.ds(start, 2048), pl.ds(pl.multiple_of(n * 256, 256), 256)], (1, 0))
        for half in range(2):
            share = out[:, half * CHUNK : (half + 1) * CHUNK]
            part[2 * n + half] = share if first else part[2 * n + half] + share
        return carry

    lax.fori_loop(*steps, body, 0)


def packed_tiles():
    return [(g, t) for g in range(36) for t in range((g * 8 + 7) // CHUNK + 1)]


def sample_kernel(
    blocks_ref, slot_ref, sketch_ref, basis_ref, projected_ref,
    tiles, matrix, operand, middle, part, other, sum_f, inbox_f, inbox2_f, totals_f,
    sum_h, inbox_h, inbox2_h, totals_h, full, full2, flat, zpart, up, down, up2, down2, gram, packed, gathered, sums, sums_z,
    power, work, right_side,
    ga_s, ga_r, gb_s, gb_r, za_s, za_r, zb_s, zb_r, ca_s, ca_r, cb_s, cb_r, fa_s, fa_r, fb_s, fb_r,
    g1_s, g1_r, g2_s, g2_r, g3_s, g3_r, local,
):
    me = Place()
    pending = []
    load = pltpu.make_async_copy(blocks_ref, tiles.at[pl.ds(0, SLOTS)], local.at[0])
    load.start()
    own = pltpu.make_async_copy(sketch_ref, operand.at[:, lanes(me.r)], local.at[1])
    own.start()
    tiles[SLOTS] = jnp.zeros((CHUNK, CHUNK), BF16)
    greet([me.col_peer(i) for i in range(1, 32)] + [me.z_peer(i) for i in range(1, NZ)])

    own.wait()

    def build(n, carry):
        start = pl.multiple_of(((n % 2) * 16 + n // 2) * CHUNK, CHUNK)
        for t in range(8):
            matrix[pl.ds(start, CHUNK), t * CHUNK : (t + 1) * CHUNK] = tiles[slot_ref[n * 8 + t]]
        return carry

    def build_some(step):
        if step == 0:
            load.wait()
        lax.fori_loop(8 * step, 8 * step + 8, build, 0)

    pending += gather_z(me, operand, (ga_s, ga_r), lambda piece: None, build_some)

    halves, more = scatter_col(
        me, part, other, sum_f, inbox_f, inbox2_f, totals_f, (ca_s, ca_r), forward(operand, matrix, part)
    )
    for copy in more:
        copy.wait_send()
    full[me.k, me.y, me.x, pl.ds(0, HALF)] = halves[0].astype(BF16)
    full[me.k, me.y, me.x, pl.ds(HALF, HALF)] = halves[1].astype(BF16)
    def own_half(rows):
        flatten(rows, flat, me.k)
        backward(me, flat, matrix, zpart, me.k, True, (0, 4))

    def other_half(steps):
        backward(me, flat, matrix, zpart, 1 - me.k, False, steps)

    hooks = (lambda: None, lambda: None, lambda: own_half(full))
    pending += gather_col(me, full, (fa_s, fa_r), hooks)
    flatten(full, flat, 1 - me.k)
    other_half((0, 2))

    def finish(piece, total):
        middle[pl.ds(piece * SUB, SUB), lanes(me.r)] = total.astype(BF16)

    def rest(step):
        if step == 0:
            other_half((2, 4))

    before, more = scatter_z(me, zpart, up, down, (za_s, za_r), finish, rest)
    pending += gather_z(me, middle, (gb_s, gb_r), before)
    for copy in more:
        copy.wait_send()

    halves, more = scatter_col(
        me, part, other, sum_h, inbox_h, inbox2_h, totals_h, (cb_s, cb_r), forward(middle, matrix, part)
    )
    pending += more
    power[pl.ds(0, HALF)] = halves[0]
    power[pl.ds(HALF, HALF)] = halves[1]
    full2[me.k, me.y, me.x, pl.ds(0, HALF)] = halves[0].astype(BF16)
    full2[me.k, me.y, me.x, pl.ds(HALF, HALF)] = halves[1].astype(BF16)

    sent = []

    def gram_part():
        gram[...] = jnp.zeros_like(gram)
        gram[:, 0:WIDTH] = dot(power[...], power[...], (1, 1), HIGHEST)
        for n, (g, t) in enumerate(packed_tiles()):
            packed[n] = gram[g * 8 : g * 8 + 8, t * CHUNK : (t + 1) * CHUNK]
        for n in range(len(packed_tiles()), PACKED):
            packed[n] = jnp.zeros((8, CHUNK), F32)
        for i in range(1, 32):
            sent.append(
                send(packed.at[pl.ds(2 * ((me.c + i) % 32), 2)], gathered.at[me.c], g1_s.at[i], g1_r.at[i], me.col_peer(i))
            )

    def gram_col():
        for copy in sent:
            copy.wait_recv()
        gathered[me.c] = packed[pl.ds(2 * me.c, 2)]
        total = gathered[0]
        for i in range(1, 32):
            total += gathered[i]
        sums_z[me.r] = total
        pending.extend(sent)
        sent.clear()
        for i in (4, 3, 5, 2, 6, 1, 7):
            sent.append(send(sums_z.at[me.r], sums_z.at[me.r], g2_s.at[i], g2_r.at[i], me.z_peer(i)))

    def gram_row():
        for copy in sent:
            copy.wait_recv()
        total = sums_z[0]
        for i in range(1, NZ):
            total += sums_z[i]
        sums[me.c] = total
        pending.extend(sent)
        sent.clear()
        for i in range(1, 32):
            sent.append(send(sums.at[me.c], sums.at[me.c], g3_s.at[i], g3_r.at[i], me.col_peer(i)))

    def gram_row_and_pass():
        gram_row()
        own_half(full2)

    pending += gather_col(me, full2, (fb_s, fb_r), (gram_part, gram_col, gram_row_and_pass))
    pending.extend(sent)
    flatten(full2, flat, 1 - me.k)
    other_half((0, 2))

    def keep(piece, total):
        right_side[piece * SUB : (piece + 1) * SUB, CHUNK:] = total

    def between(step):
        if step == 0:
            other_half((2, 4))
            for copy in sent:
                copy.wait_recv()
            unpack_gram(sums, work)
        for panel in (2 * step, 2 * step + 1):
            eliminate(work, panel)

    before, more = scatter_z(me, zpart, up2, down2, (zb_s, zb_r), keep, between)
    pending += more
    eliminate(work, 8)
    right_side[0:WIDTH, 0:CHUNK] = power[...]
    right_side[WIDTH:] = jnp.zeros((384 - WIDTH, 2 * CHUNK), F32)
    for piece in range(NSUB):
        before(piece)
    out = dot(work[0:WIDTH, 384:], right_side[...], (1, 0), HIGHEST)
    basis_ref[...] = out[:, :CHUNK]
    projected_ref[...] = out[:, CHUNK:]
    for copy in pending:
        copy.wait_send()


def over_lanes(block, lane):
    return jnp.broadcast_to(block[:, lane : lane + 1], (8, CHUNK))


def over_rows(block, row):
    return jnp.broadcast_to(block[row : row + 1, :], (8, CHUNK))


def invert_factor(left, off):
    row = lax.broadcasted_iota(jnp.int32, (8, CHUNK), 0)
    lane = lax.broadcasted_iota(jnp.int32, (8, CHUNK), 1)
    L = [left[8 * h : 8 * h + 8] for h in range(4)]
    R = [(lane == row + 8 * h + off).astype(F32) for h in range(4)]
    for g in range(4):
        cols = {h: [over_lanes(L[h], off + 8 * g + b) for b in range(8)] for h in range(g, 4)}
        p = [[over_rows(cols[g][b], a) for b in range(a + 1)] for a in range(8)]
        left_rows = [over_rows(L[g], a) for a in range(8)]
        right_rows = [over_rows(R[g], a) for a in range(8)]
        for b in range(8):
            inv = lax.rsqrt(p[b][b])
            for a in range(b + 1, 8):
                p[a][b] = p[a][b] * inv
            for a in range(b + 1, 8):
                for c in range(b + 1, a + 1):
                    p[a][c] = p[a][c] - p[a][b] * p[c][b]
            left_rows[b] = left_rows[b] * inv
            right_rows[b] = right_rows[b] * inv
            for a in range(b + 1, 8):
                left_rows[a] = left_rows[a] - p[a][b] * left_rows[b]
                right_rows[a] = right_rows[a] - p[a][b] * right_rows[b]
            for h in range(g + 1, 4):
                cols[h][b] = cols[h][b] * inv
                for a in range(b + 1, 8):
                    cols[h][a] = cols[h][a] - p[a][b] * cols[h][b]
        for h in range(g + 1, 4):
            for b in range(8):
                L[h] = L[h] - cols[h][b] * left_rows[b]
                R[h] = R[h] - cols[h][b] * right_rows[b]
        new = right_rows[0]
        for a in range(1, 8):
            new = jnp.where(row == a, right_rows[a], new)
        R[g] = new
    return jnp.concatenate(R, 0)


def unpack_gram(sums, work):
    work[...] = jnp.zeros_like(work)
    for n, (g, t) in enumerate(packed_tiles()):
        work[g * 8 : g * 8 + 8, t * CHUNK : (t + 1) * CHUNK] = sums[n // 2, n % 2] * (1.0 / 32768.0)
    work[0:128, 128:256] = work[128:256, 0:128].T
    work[0:128, 256:384] = work[256:384, 0:128].T
    work[128:256, 256:384] = work[256:384, 128:256].T
    row = lax.broadcasted_iota(jnp.int32, (CHUNK, CHUNK), 0)
    lane = lax.broadcasted_iota(jnp.int32, (CHUNK, CHUNK), 1)
    one = (row == lane).astype(F32)
    for t in range(3):
        work[t * CHUNK : (t + 1) * CHUNK, 384 + t * CHUNK : 384 + (t + 1) * CHUNK] = one


def eliminate(work, panel):
    r0 = panel * 32
    tile, off = r0 // CHUNK, r0 % CHUNK
    block = slice(tile * CHUNK, (tile + 1) * CHUNK)
    span = slice(tile * CHUNK, 384 + (tile + 1) * CHUNK)
    right = invert_factor(work[r0 : r0 + 32, block], off)
    right_high, right_low = halves_of(right)
    work_high, work_low = halves_of(work[block, span])
    both = dot(jnp.concatenate([right_high, right_low], 0), work_high, (1, 0))
    upper = both[:32] + both[32:] + dot(right_high, work_low, (1, 0))
    if panel < 8:
        none = jnp.zeros((32, CHUNK), BF16)
        thrice_high = jnp.concatenate([right_high] * 3 + [none], 0)
        thrice_low = jnp.concatenate([right_low] * 3 + [none], 0)
        below_high, below_low = halves_of(work[r0 + 32 : WIDTH, block])
        lower = dot(below_high, thrice_high, (1, 1)) + dot(below_high, thrice_low, (1, 1)) + dot(below_low, thrice_high, (1, 1))
        lower_high, lower_low = halves_of(lower)
        lane = lax.broadcasted_iota(jnp.int32, lower.shape, 1)
        mixed = jnp.where(lane < 64, lower_high.astype(F32), lower_low.astype(F32)).astype(BF16)
        upper_high, upper_low = halves_of(upper)
        zero = jnp.zeros(upper.shape, BF16)
        work[r0 + 32 : WIDTH, span] -= dot(
            mixed, jnp.concatenate([upper_high, upper_low, upper_high, zero], 0), (1, 0)
        )
    work[r0 : r0 + 32, 384 : 384 + (tile + 1) * CHUNK] = upper[:, 384 - tile * CHUNK :]


def halves_of(value):
    high = value.astype(BF16)
    return high, (value - high.astype(F32)).astype(BF16)


def sem(*shape):
    return [DMA(shape), DMA(shape)]


def local(blocks, positions, counts, sketch):
    places = positions[0, 0]
    used = lax.iota(jnp.int32, SLOTS) < counts[0, 0]
    where = jnp.where(used, places, -1)
    hit = where[None, :] == lax.iota(jnp.int32, 256)[:, None]
    slots = jnp.min(jnp.where(hit, lax.iota(jnp.int32, SLOTS)[None, :], SLOTS), axis=1)

    vmem = pl.BlockSpec(memory_space=pltpu.VMEM)
    hbm = pl.BlockSpec(memory_space=pltpu.HBM)
    smem = pl.BlockSpec(memory_space=pltpu.SMEM)
    V = pltpu.VMEM
    basis, projected = pl.pallas_call(
        sample_kernel,
        out_shape=[jax.ShapeDtypeStruct((WIDTH, CHUNK), F32)] * 2,
        in_specs=[hbm, smem, hbm],
        out_specs=[vmem, vmem],
        scratch_shapes=[
            V((SLOTS + 1, CHUNK, CHUNK), BF16),
            V((4096, 1024), BF16),
            V((WIDTH, 1024), BF16),
            V((WIDTH, 1024), BF16),
            V((2, SIDE, SIDE, WIDTH, CHUNK), F32),
            V((SIDE, SIDE, WIDTH, CHUNK), F32),
            V((SIDE, SIDE, WIDTH, CHUNK), F32),
            V((2, 3, SIDE, HALF, CHUNK), F32),
            V((2, 3, HALF, CHUNK), F32),
            V((2, SIDE, HALF, CHUNK), F32),
            V((SIDE, SIDE, WIDTH, CHUNK), BF16),
            V((2, 3, SIDE, HALF, CHUNK), BF16),
            V((2, 3, HALF, CHUNK), BF16),
            V((2, SIDE, HALF, CHUNK), BF16),
            V((2, SIDE, SIDE, WIDTH, CHUNK), BF16),
            V((2, SIDE, SIDE, WIDTH, CHUNK), BF16),
            V((WIDTH, 2048), BF16),
            V((NZ, WIDTH, CHUNK), F32),
            V((4, WIDTH, CHUNK), F32),
            V((3, WIDTH, CHUNK), F32),
            V((4, WIDTH, CHUNK), F32),
            V((3, WIDTH, CHUNK), F32),
            V((WIDTH, 384), F32),
            V((PACKED, 8, CHUNK), F32),
            V((32, 2, 8, CHUNK), F32),
            V((32, 2, 8, CHUNK), F32),
            V((NZ, 2, 8, CHUNK), F32),
            V((WIDTH, CHUNK), F32),
            V((384, 768), F32),
            V((384, 2 * CHUNK), F32),
            *sem(NSUB, 7),
            *sem(NSUB, 7),
            *sem(NSUB, 7),
            *sem(NSUB, 7),
            *sem(26),
            *sem(26),
            *sem(43),
            *sem(43),
            *sem(32),
            *sem(8),
            *sem(32),
            DMA((2,)),
        ],
        compiler_params=pltpu.CompilerParams(
            collective_id=1, has_side_effects=True, vmem_limit_bytes=52 << 20
        ),
    )(blocks[0, 0], slots, sketch.T)

    return (basis.T, projected.T)


def solution(mesh):
    return jax.shard_map(
        local,
        mesh=mesh,
        in_specs=(
            P("row", "col", None, None, None),
            P("row", "col", None),
            P("row", "col"),
            P(("col", "row"), None),
        ),
        out_specs=(P(("row", "col"), None), P(("col", "row"), None)),
        check_vma=False,
    )
```

```python
import functools

import jax
import jax.numpy as jnp
from jax import lax
from jax.experimental import pallas as pl
from jax.experimental.pallas import tpu as pltpu
from jax.sharding import PartitionSpec as P

MESH = pl.DeviceIdType.MESH
F32 = jnp.float32
BF16 = jnp.bfloat16
DMA = pltpu.SemaphoreType.DMA
HIGHEST = lax.Precision.HIGHEST

NZ = 8
SIDE = 4
CHUNK = 128
WIDTH = 288
HALF = 144
SUB = 96
NSUB = WIDTH // SUB
SLOTS = 96
PACKED = 64


class Place:
    def __init__(self):
        self.r = lax.axis_index("row")
        self.c = lax.axis_index("col")
        self.y = self.c // 8
        self.x = (self.c // 2) % SIDE
        self.k = self.c % 2

    def x_peer(self, i):
        return (self.r, (self.y * SIDE + (self.x + i) % SIDE) * 2 + self.k)

    def y_peer(self, i):
        return (self.r, (((self.y + i) % SIDE) * SIDE + self.x) * 2 + self.k)

    def sibling(self):
        return (self.r, self.c + 1 - 2 * self.k)

    def z_peer(self, i):
        return ((self.r + i) % NZ, self.c)

    def col_peer(self, i):
        return (self.r, (self.c + i) % 32)


def greet(peers):
    barrier = pltpu.get_barrier_semaphore()
    for peer in peers:
        pl.semaphore_signal(barrier, inc=1, device_id=peer, device_id_type=MESH)
    pl.semaphore_wait(barrier, len(peers))


def send(src, dst, send_sem, recv_sem, peer):
    copy = pltpu.make_async_remote_copy(
        src_ref=src,
        dst_ref=dst,
        send_sem=send_sem,
        recv_sem=recv_sem,
        device_id=peer,
        device_id_type=MESH,
    )
    copy.start()
    return copy


def lanes(chunk):
    return pl.ds(pl.multiple_of(chunk * CHUNK, CHUNK), CHUNK)


def gather_z_piece(me, full, sems, piece, pending):
    rows = pl.ds(piece * SUB, SUB)
    send_sem, recv_sem = sems

    def go(step, way):
        owner = (me.r - way * step + NZ) % NZ
        block = full.at[rows, lanes(owner)]
        n = (0 if way == 1 else 4) + step
        copy = send(block, block, send_sem.at[piece, n], recv_sem.at[piece, n], me.z_peer(way % NZ))
        pending.append(copy)
        return copy

    return go


def gather_z(me, full, sems, before, meanwhile=None):
    pending = []
    goes = [gather_z_piece(me, full, sems, piece, pending) for piece in range(NSUB)]
    held = {}
    for step in range(4):
        for piece in range(NSUB):
            if step > 0:
                for copy in held[piece]:
                    copy.wait_recv()
            else:
                before(piece)
            copies = [goes[piece](step, 1)]
            if step < 3:
                copies.append(goes[piece](step, -1))
            held[piece] = copies
        if meanwhile is not None:
            meanwhile(step)
    for piece in range(NSUB):
        for copy in held[piece]:
            copy.wait_recv()
    return pending


def scatter_z(me, part, up, down, sems, finish, between=lambda step: None):
    send_sem, recv_sem = sems
    pending = []
    held = {}
    for step in range(4):
        for piece in range(NSUB):
            rows = pl.ds(piece * SUB, SUB)
            copies = []
            target = (me.r + 4 + step) % NZ
            if step == 0:
                src = part.at[target, rows]
            else:
                held[piece][0].wait_recv()
                src = up.at[step - 1, rows]
                src[...] += part[target, rows]
            copies.append(
                send(src, up.at[step, rows], send_sem.at[piece, step], recv_sem.at[piece, step], me.z_peer(NZ - 1))
            )
            if step < 3:
                target = (me.r + 3 - step) % NZ
                if step == 0:
                    src = part.at[target, rows]
                else:
                    held[piece][1].wait_recv()
                    src = down.at[step - 1, rows]
                    src[...] += part[target, rows]
                copies.append(
                    send(
                        src, down.at[step, rows], send_sem.at[piece, 4 + step], recv_sem.at[piece, 4 + step], me.z_peer(1)
                    )
                )
            else:
                copies.append(held[piece][1])
            held[piece] = copies
            pending.extend(copies if step < 3 else copies[:1])
        between(step)

    def before(piece):
        rows = pl.ds(piece * SUB, SUB)
        held[piece][0].wait_recv()
        held[piece][1].wait_recv()
        finish(piece, part[me.r, rows] + up[3, rows] + down[2, rows])

    return before, pending


def scatter_col(me, part, other, summed, relay_x, relay_y, inbox, inbox2, totals, sems, compute):
    send_sem, recv_sem = sems
    pending = []
    order = [(me.y + i) % SIDE for i in (1, 2, 3, 0)]
    crossing = []
    for i, y in enumerate(order):
        compute(1 - me.k, y)
        crossing.append(send(part.at[1 - me.k, y], other.at[y], send_sem.at[i], recv_sem.at[i], me.sibling()))
    for y in order:
        compute(me.k, y)
    pending.extend(crossing)
    low, high = pl.ds(0, HALF), pl.ds(HALF, HALF)
    def start(n, src, dst, peer):
        copy = send(src, dst, send_sem.at[n], recv_sem.at[n], peer)
        pending.append(copy)
        return copy

    def add_to(ref, own):
        ref[...] = (ref[...].astype(F32) + own.astype(F32)).astype(ref.dtype)

    ways = (1, 3, 1, 3)
    far_x, near_x = [], []
    for i, y in enumerate(order):
        crossing[i].wait_recv()
        for x in range(SIDE):
            summed[y, x] = (part[me.k, y, x] + other[y, x]).astype(summed.dtype)
        far_x.append(start(7 + 3 * i, summed.at[y, (me.x + 2) % SIDE, low], relay_x.at[i], me.x_peer(ways[i])))
        back = 4 - ways[i]
        near_x.append(
            start(8 + 3 * i, summed.at[y, (me.x + back) % SIDE, low], inbox.at[0, 1, i], me.x_peer(back))
        )
        if i == 0:
            near_y = [start(4, summed.at[y, pl.ds(2, 2), high], inbox.at[1, 0, pl.ds(2, 2)], me.y_peer(1))]
        if i == 1:
            far_y = [
                start(5, summed.at[y, pl.ds(0, 2), high], relay_y.at[0], me.y_peer(1)),
                start(6, summed.at[y, pl.ds(2, 2), high], relay_y.at[1], me.y_peer(3)),
            ]
        if i == 2:
            near_y.append(start(26, summed.at[y, pl.ds(0, 2), high], inbox.at[1, 1, pl.ds(0, 2)], me.y_peer(3)))
    passed_x, passed_y = [], []
    for i, y in enumerate(order):
        far_x[i].wait_recv()
        add_to(relay_x.at[i], summed[y, (me.x + ways[i]) % SIDE, low])
        passed_x.append(start(9 + 3 * i, relay_x.at[i], inbox.at[0, 0, i], me.x_peer(ways[i])))
        if i in (1, 2):
            h = i - 1
            far_y[h].wait_recv()
            add_to(relay_y.at[h], summed[(me.y + ways[h]) % SIDE, pl.ds(2 * h, 2), high])
            passed_y.append(
                start(27 + h, relay_y.at[h], inbox.at[1, h, pl.ds(2 * h, 2)], me.y_peer(ways[h]))
            )
    second = []
    for i, y in enumerate(order):
        near_x[i].wait_recv()
        passed_x[i].wait_recv()
        total = summed[y, me.x, low].astype(F32) + inbox[0, 0, i].astype(F32) + inbox[0, 1, i].astype(F32)
        totals[0, y] = total.astype(totals.dtype)
        if i < 3:
            second.append(start(20 + i, totals.at[0, y], inbox2.at[0, i], me.y_peer(i + 1)))
    for copy in near_y + passed_y:
        copy.wait_recv()
    for i in (2, 1, 3, 0):
        x = (me.x + i) % SIDE
        total = summed[me.y, x, high].astype(F32) + inbox[1, 0, x].astype(F32) + inbox[1, 1, x].astype(F32)
        totals[1, x] = total.astype(totals.dtype)
        if i:
            second.append(start(22 + i, totals.at[1, x], inbox2.at[1, i - 1], me.x_peer(i)))
    for copy in second:
        copy.wait_recv()
    halves = []
    for h, mine in enumerate((me.y, me.x)):
        total = totals[h, mine].astype(F32)
        for j in range(3):
            total += inbox2[h, j].astype(F32)
        halves.append(total)
    return halves, pending


def gather_col(me, full, sems, between=(lambda: None, lambda: None, lambda: None)):
    send_sem, recv_sem = sems
    pending = []
    k, y, x = me.k, me.y, me.x
    low, high = pl.ds(0, HALF), pl.ds(HALF, HALF)
    own_low, own_high = full.at[k, y, x, low], full.at[k, y, x, high]
    count = [0]

    def start(block, peer):
        n = count[0]
        count[0] += 1
        copy = send(block, block, send_sem.at[n], recv_sem.at[n], peer)
        pending.append(copy)
        return copy

    first = {i: (start(own_low, me.y_peer(i)), start(own_high, me.x_peer(i))) for i in (1, 3, 2)}
    second = {i: [start(own_low, me.x_peer(i)), start(own_high, me.y_peer(i))] for i in (1, 2, 3)}
    third = [start(full.at[k, y, x], me.sibling())]
    between[0]()
    for i in (1, 3, 2):
        first[i][0].wait_recv()
        block = full.at[k, (y - i + SIDE) % SIDE, x, low]
        for j in (2, 1, 3):
            second[j].append(start(block, me.x_peer(j)))
        third.append(start(block, me.sibling()))
        first[i][1].wait_recv()
        block = full.at[k, y, (x - i + SIDE) % SIDE, high]
        for j in (2, 1, 3):
            second[j].append(start(block, me.y_peer(j)))
        third.append(start(block, me.sibling()))
    between[1]()
    for i in (1, 3, 2):
        for copy in second[i]:
            copy.wait_recv()
        third.append(start(full.at[k, :, (x - i + SIDE) % SIDE, low], me.sibling()))
        third.append(start(full.at[k, (y - i + SIDE) % SIDE, :, high], me.sibling()))
    between[2]()
    for copy in third:
        copy.wait_recv()
    return pending


def dot(a, b, contract, precision=None):
    return lax.dot_general(a, b, ((contract[:1], contract[1:]), ((), ())), precision=precision, preferred_element_type=F32)


def forward(operand, matrix, part):
    def compute(core, y):
        for half in range(2):
            start = pl.multiple_of((core * 16 + y * 4 + half * 2) * CHUNK, 256)
            out = dot(operand[...], matrix[pl.ds(start, 256), :], (1, 1))
            part[core, y, 2 * half] = out[:, :CHUNK]
            part[core, y, 2 * half + 1] = out[:, CHUNK:]

    return compute


def flatten(full, flat, core):
    def body(n, carry):
        flat[:, pl.ds(pl.multiple_of(n * CHUNK, CHUNK), CHUNK)] = full[core, n // SIDE, n % SIDE]
        return carry

    lax.fori_loop(0, 16, body, 0)


def backward(me, flat, matrix, part, core, first, steps):
    start = pl.multiple_of(core * 2048, 2048)

    def body(step, carry):
        n = (me.r // 2 + 6 - step) % 4
        out = dot(flat[...], matrix[pl.ds(start, 2048), pl.ds(pl.multiple_of(n * 256, 256), 256)], (1, 0))
        for half in range(2):
            share = out[:, half * CHUNK : (half + 1) * CHUNK]
            part[2 * n + half] = share if first else part[2 * n + half] + share
        return carry

    lax.fori_loop(*steps, body, 0)


def packed_tiles():
    return [(g, t) for g in range(36) for t in range((g * 8 + 7) // CHUNK + 1)]


def sample_kernel(
    blocks_ref, slot_ref, sketch_ref, basis_ref, projected_ref,
    tiles, matrix, operand, middle, part, other, sum_f, relay_x_f, relay_y_f, inbox_f, inbox2_f, totals_f,
    sum_h, relay_x_h, relay_y_h, inbox_h, inbox2_h, totals_h, full, full2, flat, zpart, up, down, up2, down2, gram, packed, gathered, sums, sums_z,
    power, work, right_side,
    ga_s, ga_r, gb_s, gb_r, za_s, za_r, zb_s, zb_r, ca_s, ca_r, cb_s, cb_r, fa_s, fa_r, fb_s, fb_r,
    g1_s, g1_r, g2_s, g2_r, g3_s, g3_r, local,
):
    me = Place()
    pending = []

    def drain():
        for copy in pending:
            copy.wait_send()
        pending.clear()

    load = pltpu.make_async_copy(blocks_ref, tiles.at[pl.ds(0, SLOTS)], local.at[0])
    load.start()
    own = pltpu.make_async_copy(sketch_ref, operand.at[:, lanes(me.r)], local.at[1])
    own.start()
    tiles[SLOTS] = jnp.zeros((CHUNK, CHUNK), BF16)
    greet([me.col_peer(i) for i in range(1, 32)] + [me.z_peer(i) for i in range(1, NZ)])

    own.wait()

    def build(n, carry):
        start = pl.multiple_of(((n % 2) * 16 + n // 2) * CHUNK, CHUNK)
        for t in range(8):
            matrix[pl.ds(start, CHUNK), t * CHUNK : (t + 1) * CHUNK] = tiles[slot_ref[n * 8 + t]]
        return carry

    def build_some(step):
        if step == 0:
            load.wait()
        lax.fori_loop(8 * step, 8 * step + 8, build, 0)

    pending += gather_z(me, operand, (ga_s, ga_r), lambda piece: None, build_some)

    halves, more = scatter_col(
        me, part, other, sum_f, relay_x_f, relay_y_f, inbox_f, inbox2_f, totals_f, (ca_s, ca_r), forward(operand, matrix, part)
    )
    pending += more
    full[me.k, me.y, me.x, pl.ds(0, HALF)] = halves[0].astype(BF16)
    full[me.k, me.y, me.x, pl.ds(HALF, HALF)] = halves[1].astype(BF16)
    def own_half(rows):
        flatten(rows, flat, me.k)
        backward(me, flat, matrix, zpart, me.k, True, (0, 4))

    def other_half(steps):
        backward(me, flat, matrix, zpart, 1 - me.k, False, steps)

    hooks = (drain, lambda: None, lambda: own_half(full))
    pending += gather_col(me, full, (fa_s, fa_r), hooks)
    flatten(full, flat, 1 - me.k)
    other_half((0, 2))

    def finish(piece, total):
        middle[pl.ds(piece * SUB, SUB), lanes(me.r)] = total.astype(BF16)

    def rest(step):
        if step == 0:
            other_half((2, 4))
            drain()

    before, more = scatter_z(me, zpart, up, down, (za_s, za_r), finish, rest)
    pending += gather_z(me, middle, (gb_s, gb_r), before)
    pending += more

    halves, more = scatter_col(
        me, part, other, sum_h, relay_x_h, relay_y_h, inbox_h, inbox2_h, totals_h, (cb_s, cb_r), forward(middle, matrix, part)
    )
    pending += more
    power[pl.ds(0, HALF)] = halves[0]
    power[pl.ds(HALF, HALF)] = halves[1]
    full2[me.k, me.y, me.x, pl.ds(0, HALF)] = halves[0].astype(BF16)
    full2[me.k, me.y, me.x, pl.ds(HALF, HALF)] = halves[1].astype(BF16)

    sent = []

    def gram_part():
        gram[...] = jnp.zeros_like(gram)
        gram[:, 0:WIDTH] = dot(power[...], power[...], (1, 1), HIGHEST)
        for n, (g, t) in enumerate(packed_tiles()):
            packed[n] = gram[g * 8 : g * 8 + 8, t * CHUNK : (t + 1) * CHUNK]
        for n in range(len(packed_tiles()), PACKED):
            packed[n] = jnp.zeros((8, CHUNK), F32)
        for i in range(1, 32):
            sent.append(
                send(packed.at[pl.ds(2 * ((me.c + i) % 32), 2)], gathered.at[me.c], g1_s.at[i], g1_r.at[i], me.col_peer(i))
            )
        drain()

    def gram_col():
        for copy in sent:
            copy.wait_recv()
        gathered[me.c] = packed[pl.ds(2 * me.c, 2)]
        total = gathered[0]
        for i in range(1, 32):
            total += gathered[i]
        sums_z[me.r] = total
        pending.extend(sent)
        sent.clear()
        for i in (4, 3, 5, 2, 6, 1, 7):
            sent.append(send(sums_z.at[me.r], sums_z.at[me.r], g2_s.at[i], g2_r.at[i], me.z_peer(i)))

    def gram_row():
        for copy in sent:
            copy.wait_recv()
        total = sums_z[0]
        for i in range(1, NZ):
            total += sums_z[i]
        sums[me.c] = total
        pending.extend(sent)
        sent.clear()
        for i in range(1, 32):
            sent.append(send(sums.at[me.c], sums.at[me.c], g3_s.at[i], g3_r.at[i], me.col_peer(i)))

    def gram_row_and_pass():
        gram_row()
        own_half(full2)

    pending += gather_col(me, full2, (fb_s, fb_r), (gram_part, gram_col, gram_row_and_pass))
    pending.extend(sent)
    flatten(full2, flat, 1 - me.k)
    other_half((0, 2))

    def keep(piece, total):
        right_side[piece * SUB : (piece + 1) * SUB, CHUNK:] = total

    def between(step):
        if step == 0:
            other_half((2, 4))
            for copy in sent:
                copy.wait_recv()
            unpack_gram(sums, work)
        for panel in (2 * step, 2 * step + 1):
            eliminate(work, panel)
        if step == 2:
            drain()

    before, more = scatter_z(me, zpart, up2, down2, (zb_s, zb_r), keep, between)
    pending += more
    eliminate(work, 8)
    right_side[0:WIDTH, 0:CHUNK] = power[...]
    right_side[WIDTH:] = jnp.zeros((384 - WIDTH, 2 * CHUNK), F32)
    for piece in range(NSUB):
        before(piece)
    drain()
    out = dot(work[0:WIDTH, 384:], right_side[...], (1, 0), HIGHEST)
    basis_ref[...] = out[:, :CHUNK]
    projected_ref[...] = out[:, CHUNK:]


def over_lanes(block, lane):
    return jnp.broadcast_to(block[:, lane : lane + 1], (8, CHUNK))


def over_rows(block, row):
    return jnp.broadcast_to(block[row : row + 1, :], (8, CHUNK))


def invert_factor(left, off):
    row = lax.broadcasted_iota(jnp.int32, (8, CHUNK), 0)
    lane = lax.broadcasted_iota(jnp.int32, (8, CHUNK), 1)
    L = [left[8 * h : 8 * h + 8] for h in range(4)]
    R = [(lane == row + 8 * h + off).astype(F32) for h in range(4)]
    for g in range(4):
        cols = {h: [over_lanes(L[h], off + 8 * g + b) for b in range(8)] for h in range(g, 4)}
        p = [[over_rows(cols[g][b], a) for b in range(a + 1)] for a in range(8)]
        left_rows = [over_rows(L[g], a) for a in range(8)]
        right_rows = [over_rows(R[g], a) for a in range(8)]
        for b in range(8):
            inv = lax.rsqrt(p[b][b])
            for a in range(b + 1, 8):
                p[a][b] = p[a][b] * inv
            for a in range(b + 1, 8):
                for c in range(b + 1, a + 1):
                    p[a][c] = p[a][c] - p[a][b] * p[c][b]
            left_rows[b] = left_rows[b] * inv
            right_rows[b] = right_rows[b] * inv
            for a in range(b + 1, 8):
                left_rows[a] = left_rows[a] - p[a][b] * left_rows[b]
                right_rows[a] = right_rows[a] - p[a][b] * right_rows[b]
            for h in range(g + 1, 4):
                cols[h][b] = cols[h][b] * inv
                for a in range(b + 1, 8):
                    cols[h][a] = cols[h][a] - p[a][b] * cols[h][b]
        for h in range(g + 1, 4):
            for b in range(8):
                L[h] = L[h] - cols[h][b] * left_rows[b]
                R[h] = R[h] - cols[h][b] * right_rows[b]
        new = right_rows[0]
        for a in range(1, 8):
            new = jnp.where(row == a, right_rows[a], new)
        R[g] = new
    return jnp.concatenate(R, 0)


def unpack_gram(sums, work):
    work[...] = jnp.zeros_like(work)
    for n, (g, t) in enumerate(packed_tiles()):
        work[g * 8 : g * 8 + 8, t * CHUNK : (t + 1) * CHUNK] = sums[n // 2, n % 2] * (1.0 / 32768.0)
    work[0:128, 128:256] = work[128:256, 0:128].T
    work[0:128, 256:384] = work[256:384, 0:128].T
    work[128:256, 256:384] = work[256:384, 128:256].T
    row = lax.broadcasted_iota(jnp.int32, (CHUNK, CHUNK), 0)
    lane = lax.broadcasted_iota(jnp.int32, (CHUNK, CHUNK), 1)
    one = (row == lane).astype(F32)
    for t in range(3):
        work[t * CHUNK : (t + 1) * CHUNK, 384 + t * CHUNK : 384 + (t + 1) * CHUNK] = one


def eliminate(work, panel):
    r0 = panel * 32
    tile, off = r0 // CHUNK, r0 % CHUNK
    block = slice(tile * CHUNK, (tile + 1) * CHUNK)
    span = slice(tile * CHUNK, 384 + (tile + 1) * CHUNK)
    right = invert_factor(work[r0 : r0 + 32, block], off)
    right_high, right_low = halves_of(right)
    work_high, work_low = halves_of(work[block, span])
    both = dot(jnp.concatenate([right_high, right_low], 0), work_high, (1, 0))
    upper = both[:32] + both[32:] + dot(right_high, work_low, (1, 0))
    if panel < 8:
        none = jnp.zeros((32, CHUNK), BF16)
        thrice_high = jnp.concatenate([right_high] * 3 + [none], 0)
        thrice_low = jnp.concatenate([right_low] * 3 + [none], 0)
        below_high, below_low = halves_of(work[r0 + 32 : WIDTH, block])
        lower = dot(below_high, thrice_high, (1, 1)) + dot(below_high, thrice_low, (1, 1)) + dot(below_low, thrice_high, (1, 1))
        lower_high, lower_low = halves_of(lower)
        lane = lax.broadcasted_iota(jnp.int32, lower.shape, 1)
        mixed = jnp.where(lane < 64, lower_high.astype(F32), lower_low.astype(F32)).astype(BF16)
        upper_high, upper_low = halves_of(upper)
        zero = jnp.zeros(upper.shape, BF16)
        work[r0 + 32 : WIDTH, span] -= dot(
            mixed, jnp.concatenate([upper_high, upper_low, upper_high, zero], 0), (1, 0)
        )
    work[r0 : r0 + 32, 384 : 384 + (tile + 1) * CHUNK] = upper[:, 384 - tile * CHUNK :]


def halves_of(value):
    high = value.astype(BF16)
    return high, (value - high.astype(F32)).astype(BF16)


def sem(*shape):
    return [DMA(shape), DMA(shape)]


def local(blocks, positions, counts, sketch):
    places = positions[0, 0]
    number = lax.broadcasted_iota(jnp.int32, (256, SLOTS), 1)
    hit = places[None, :] == lax.broadcasted_iota(jnp.int32, (256, SLOTS), 0)
    slots = jnp.min(jnp.where(hit & (number < counts[0, 0]), number, SLOTS), axis=1)

    vmem = pl.BlockSpec(memory_space=pltpu.VMEM)
    hbm = pl.BlockSpec(memory_space=pltpu.HBM)
    smem = pl.BlockSpec(memory_space=pltpu.SMEM)
    V = pltpu.VMEM
    basis, projected = pl.pallas_call(
        sample_kernel,
        out_shape=[jax.ShapeDtypeStruct((WIDTH, CHUNK), F32)] * 2,
        in_specs=[hbm, smem, hbm],
        out_specs=[vmem, vmem],
        scratch_shapes=[
            V((SLOTS + 1, CHUNK, CHUNK), BF16),
            V((4096, 1024), BF16),
            V((WIDTH, 1024), BF16),
            V((WIDTH, 1024), BF16),
            V((2, SIDE, SIDE, WIDTH, CHUNK), F32),
            V((SIDE, SIDE, WIDTH, CHUNK), F32),
            V((SIDE, SIDE, WIDTH, CHUNK), F32),
            V((SIDE, HALF, CHUNK), F32),
            V((2, 2, HALF, CHUNK), F32),
            V((2, 2, SIDE, HALF, CHUNK), F32),
            V((2, 3, HALF, CHUNK), F32),
            V((2, SIDE, HALF, CHUNK), F32),
            V((SIDE, SIDE, WIDTH, CHUNK), BF16),
            V((SIDE, HALF, CHUNK), BF16),
            V((2, 2, HALF, CHUNK), BF16),
            V((2, 2, SIDE, HALF, CHUNK), BF16),
            V((2, 3, HALF, CHUNK), BF16),
            V((2, SIDE, HALF, CHUNK), BF16),
            V((2, SIDE, SIDE, WIDTH, CHUNK), BF16),
            V((2, SIDE, SIDE, WIDTH, CHUNK), BF16),
            V((WIDTH, 2048), BF16),
            V((NZ, WIDTH, CHUNK), F32),
            V((4, WIDTH, CHUNK), F32),
            V((3, WIDTH, CHUNK), F32),
            V((4, WIDTH, CHUNK), F32),
            V((3, WIDTH, CHUNK), F32),
            V((WIDTH, 384), F32),
            V((PACKED, 8, CHUNK), F32),
            V((32, 2, 8, CHUNK), F32),
            V((32, 2, 8, CHUNK), F32),
            V((NZ, 2, 8, CHUNK), F32),
            V((WIDTH, CHUNK), F32),
            V((384, 768), F32),
            V((384, 2 * CHUNK), F32),
            *sem(NSUB, 7),
            *sem(NSUB, 7),
            *sem(NSUB, 7),
            *sem(NSUB, 7),
            *sem(29),
            *sem(29),
            *sem(43),
            *sem(43),
            *sem(32),
            *sem(8),
            *sem(32),
            DMA((2,)),
        ],
        compiler_params=pltpu.CompilerParams(
            collective_id=1, has_side_effects=True, vmem_limit_bytes=52 << 20
        ),
    )(blocks[0, 0], slots, sketch.T)

    return (basis.T, projected.T)


def solution(mesh):
    return jax.shard_map(
        local,
        mesh=mesh,
        in_specs=(
            P("row", "col", None, None, None),
            P("row", "col", None),
            P("row", "col"),
            P(("col", "row"), None),
        ),
        out_specs=(P(("row", "col"), None), P(("col", "row"), None)),
        check_vma=False,
    )
```
